256 devices in a mesh: az: 32 (over y, z_lo, x), ax: 8 (over z_hi, core).
Axes of the slice: x: 4, y: 4, z: 8 (z_hi: 4, z_lo: 2; z = z_hi * 2 + z_lo), core: 2. Of those that a mesh axis runs over, the one named last changes fastest.
Arguments:
- state: float32 [5, 32, 512, 1024], P(None, 'ax', 'az'), may hold values from -6 to 6
- block_inverse: float32 [5, 5, 1024], replicated, may hold values from -0.1 to 0.4, as said below
- coupling: float32 [1024], replicated, may hold values from 0.3 to 0.9
- diffusion: float32 [5], replicated, may hold values from 0.05 to 0.45
Outputs:
- solution: float32 [5, 32, 512, 1024], P(None, 'ax', 'az')
The draws below stay inside these ranges and needn't reach their ends.
Inputs may be any that keep to these rules, and one draw needn't show every extreme that they name: `block_inverse`: each matrix has diagonal entries between 0.2 and 0.4 and off-diagonal entries of magnitude at most 0.1.
All inputs are finite; a program needn't handle non-finite values.
Results may differ from the reference program's by a relative error of at most 0.0001.
Values sent between devices are 32-bit elements; how exact they have to be, the bound alone decides.
No kernel may reach another device: no remote copies, remote signals or barrier semaphores. Data moves between devices by JAX's collectives and lax.ppermute only.
A program may use at most 64 MiB of HBM per device.

```python
import math
import jax
import jax.numpy as jnp
from jax import lax

NR = 1024
VARS = 5
CYCLES = 8
MODE_STEP = 8
ITERS = 4
NT = 512
NZ = 32


def draw_block_inverse(key, part):
    key = jax.random.fold_in(key, 7)
    key_off, key_diag = jax.random.split(key)
    spread = 0.08
    offdiag = jax.random.uniform(key_off, (VARS, VARS, NR), jnp.float32, -spread, spread)
    diagonal = jax.random.uniform(key_diag, (VARS, NR), jnp.float32, 0.2, 0.4)
    identity = jnp.eye(VARS, dtype=jnp.float32)[:, :, None]
    return offdiag * (1.0 - identity) + identity * diagonal[None, :, :]


def block_scale(own_key, shape, cuts, low, high):
    factor_of, own = 1.0, jax.random.fold_in(own_key, 6)
    for axis_at, shards_of in cuts:
        heights = jnp.exp(jax.random.uniform(jax.random.fold_in(own, axis_at), (shards_of,), jnp.float32, low / len(cuts), high / len(cuts)))
        factor_of = factor_of * jnp.repeat(heights, shape[axis_at] // shards_of).reshape([-1 if axis == axis_at else 1 for axis in range(len(shape))])
    return factor_of


def centred(stream_key, extent, deviation, most, cuts=(), kind=jnp.bfloat16):
    array = deviation * jax.random.normal(stream_key, extent, jnp.float32)
    if cuts:
        array = array * block_scale(stream_key, extent, cuts, -0.22, 0.18)
    return jnp.clip(array, -most, most).astype(kind)


def setup_inputs(seed: int = 0) -> dict:
    key_list = jax.random.split(jax.random.key(seed), 5)
    state = centred(key_list[0], (VARS, NZ, NT, NR), 1.0, 6.0, ((1, 8), (2, 32)), jnp.float32)
    block_inverse = draw_block_inverse(jax.random.fold_in(key_list[4], 71), 0)
    coupling = jnp.clip(jnp.exp(jax.random.uniform(key_list[2], (NR,), jnp.float32, math.log(0.3), math.log(0.9))), 0.3, 0.9)
    diffusion = jnp.clip(jnp.exp(jax.random.uniform(key_list[3], (VARS,), jnp.float32, math.log(0.05), math.log(0.45))), 0.05, 0.45)
    return dict(state=state, block_inverse=block_inverse, coupling=coupling, diffusion=diffusion)


def fourier_table(first, count, period, modes):
    angles = first + jnp.arange(count, dtype=jnp.int32)
    orders = jnp.arange(modes, dtype=jnp.int32)
    phase = ((angles[:, None] * orders[None, :]) % period).astype(jnp.float32) * (2.0 * jnp.pi / period)
    return jnp.concatenate([jnp.cos(phase), jnp.sin(phase)], axis=1)


def mode_scale(modes, period):
    orders = jnp.arange(modes, dtype=jnp.int32)
    weights = jnp.where(orders == 0, 1.0 / period, 2.0 / period).astype(jnp.float32)
    weights = jnp.concatenate([weights, weights])
    cycles_idx = jnp.arange(CYCLES, dtype=jnp.int32)
    both = jnp.concatenate([orders, orders])
    keep = (both[None, :] < (cycles_idx[:, None] + 1) * MODE_STEP).astype(jnp.float32)
    return keep * weights[None, :]


def reference(state, block_inverse, coupling, diffusion):
    modes = CYCLES * MODE_STEP
    table = fourier_table(0, NT, NT, modes)
    scaling = mode_scale(modes, NT)
    zero_plane = jnp.zeros_like(state[:, :1])
    above = jnp.concatenate([state[:, 1:], zero_plane], axis=1)
    below = jnp.concatenate([zero_plane, state[:, :-1]], axis=1)
    forcing = state + diffusion[:, None, None, None] * (above - 2.0 * state + below)

    def solve_plane(plane):
        solution = jnp.zeros_like(plane)
        for sweep_index in range(ITERS):
            partner = jnp.roll(solution[:, :, 0], NT // 2, axis=1)
            left = jnp.concatenate([partner[:, :, None], solution[:, :, :-1]], axis=2)
            right = jnp.concatenate([solution[:, :, 1:], jnp.zeros_like(solution[:, :, :1])], axis=2)
            source = plane + coupling * (left + right)
            solution = jnp.sum(block_inverse[:, :, None, :] * source[None], axis=1)
            inner = jnp.swapaxes(solution[:, :, :CYCLES], 1, 2)
            coefficients = jnp.einsum("vkt,tj->vkj", inner, table, precision=lax.Precision.HIGHEST)
            coefficients = coefficients * scaling[None]
            smooth = jnp.einsum("vkj,tj->vkt", coefficients, table, precision=lax.Precision.HIGHEST)
            solution = jnp.concatenate([jnp.swapaxes(smooth, 1, 2), solution[:, :, CYCLES:]], axis=2)
        return solution

    planes_first = jnp.swapaxes(forcing, 0, 1)
    solved = lax.map(solve_plane, planes_first)
    return jnp.swapaxes(solved, 0, 1)
```

```python
import functools

import jax
import jax.numpy as jnp
import numpy as np
from jax import lax
from jax.experimental import pallas as pl
from jax.experimental.pallas import tpu as pltpu
from jax.sharding import PartitionSpec as P

CYCLES = 8
MODE_STEP = 8
MODES = CYCLES * MODE_STEP
COLUMNS = 2 * MODES
ITERS = 4
REACH = CYCLES + ITERS - 1
SLOT = 12
PLANE = 64
HIGHEST = lax.Precision.HIGHEST
VMEM_LIMIT = 48 * 1024 * 1024


def fourier_tables(period):
    angles = np.arange(period)[:, None]
    orders = np.arange(MODES)[None, :]
    phase = (angles * orders % period) * (2.0 * np.pi / period)
    table = np.concatenate([np.cos(phase), np.sin(phase)], axis=1)
    weights = np.where(np.arange(MODES) == 0, 1.0 / period, 2.0 / period)
    weights = np.concatenate([weights, weights])
    return table.astype(np.float32), (table * weights).T.astype(np.float32)


def pack_kernel(inner_ref, state_ref, packed_ref, first_ref, last_ref, sems):
    variables, planes = inner_ref.shape[:2]
    first = pltpu.make_async_copy(state_ref.at[:, 0:1], first_ref, sems.at[0])
    last = pltpu.make_async_copy(state_ref.at[:, planes - 1 : planes], last_ref, sems.at[1])
    first.start()
    last.start()
    lane = lax.broadcasted_iota(jnp.int32, inner_ref.shape[2:], 1)
    for pair in range(planes // 2):
        total = jnp.zeros(inner_ref.shape[2:], jnp.float32)
        for part in range(2):
            for v in range(variables):
                block = jnp.where(lane < REACH, inner_ref[v, 2 * pair + part], 0.0)
                shift = part * PLANE + v * SLOT
                total = total + (pltpu.roll(block, shift, 1) if shift else block)
        for target in range(packed_ref.shape[0]):
            packed_ref[target, :, pair * 128 : pair * 128 + 128] = total
    first.wait()
    last.wait()


def pack(state, devices):
    variables, planes, angles, radii = state.shape
    edge = jax.ShapeDtypeStruct((variables, 1, angles, radii), jnp.float32)
    return pl.pallas_call(
        pack_kernel,
        grid=(1,),
        out_shape=[
            jax.ShapeDtypeStruct((devices, angles, planes * PLANE), jnp.float32),
            edge,
            edge,
        ],
        in_specs=[
            pl.BlockSpec((variables, planes, angles, 128), lambda i: (0, 0, 0, 0)),
            pl.BlockSpec(memory_space=pl.ANY),
        ],
        out_specs=[
            pl.BlockSpec((devices, angles, planes * PLANE), lambda i: (0, 0, 0)),
            pl.BlockSpec(memory_space=pl.ANY),
            pl.BlockSpec(memory_space=pl.ANY),
        ],
        scratch_shapes=[pltpu.SemaphoreType.DMA((2,))],
        compiler_params=pltpu.CompilerParams(vmem_limit_bytes=VMEM_LIMIT),
        name="pack",
    )(state, state)


def transform_kernel(table_ref, gathered_ref, modes_ref, first_ref, last_ref):
    whole = gathered_ref[...].reshape(-1, gathered_ref.shape[2])
    modes = jnp.dot(
        table_ref[...], whole, precision=HIGHEST, preferred_element_type=jnp.float32
    ).T
    modes_ref[...] = modes
    first_ref[...] = modes[:PLANE]
    last_ref[...] = modes[modes.shape[0] - PLANE :]


def transform(table, gathered):
    rows = gathered.shape[2]
    edge = jax.ShapeDtypeStruct((PLANE, COLUMNS), jnp.float32)
    return pl.pallas_call(
        transform_kernel,
        out_shape=[jax.ShapeDtypeStruct((rows, COLUMNS), jnp.float32), edge, edge],
        compiler_params=pltpu.CompilerParams(vmem_limit_bytes=VMEM_LIMIT),
        name="transform",
    )(table, gathered)


def outer_kernel(
    diffusion_ref, state_ref, below_ref, above_ref, inverse_ref, coupling_ref, out_ref,
    start_ref, step_ref,
):
    variables, planes, _, radii = state_ref.shape
    radius = lax.broadcasted_iota(jnp.int32, (variables, radii), 1)
    for u in range(variables):
        rows = jnp.where(radius < CYCLES, 0.0, inverse_ref[u])
        start_ref[u] = rows
        step_ref[u] = rows * coupling_ref[...]

    def mixed(ref, source):
        return [
            sum(ref[u, v : v + 1, :] * source[v] for v in range(variables))
            for u in range(variables)
        ]

    for z in range(planes):
        forcing = []
        for v in range(variables):
            here = state_ref[v, z]
            below = below_ref[v, 0] if z == 0 else state_ref[v, z - 1]
            above = above_ref[v, 0] if z == planes - 1 else state_ref[v, z + 1]
            forcing.append(here + diffusion_ref[v] * (above - 2.0 * here + below))
        first = mixed(start_ref, forcing)
        solution = first
        for _ in range(ITERS - 1):
            pair = [pltpu.roll(s, 1, 1) + pltpu.roll(s, radii - 1, 1) for s in solution]
            solution = [a + b for a, b in zip(first, mixed(step_ref, pair))]
        for v in range(variables):
            out_ref[v, z] = solution[v]


def outer(state, below, above, block_inverse, coupling, diffusion):
    variables, planes, angles, radii = state.shape
    block = 8
    return pl.pallas_call(
        outer_kernel,
        grid=(angles // block,),
        out_shape=jax.ShapeDtypeStruct(state.shape, jnp.float32),
        in_specs=[
            pl.BlockSpec(memory_space=pltpu.SMEM),
            pl.BlockSpec((variables, planes, block, radii), lambda i: (0, 0, i, 0)),
            pl.BlockSpec((variables, 1, block, radii), lambda i: (0, 0, i, 0)),
            pl.BlockSpec((variables, 1, block, radii), lambda i: (0, 0, i, 0)),
            pl.BlockSpec((variables, variables, radii), lambda i: (0, 0, 0)),
            pl.BlockSpec((1, radii), lambda i: (0, 0)),
        ],
        out_specs=pl.BlockSpec((variables, planes, block, radii), lambda i: (0, 0, i, 0)),
        scratch_shapes=[
            pltpu.VMEM((variables, variables, radii), jnp.float32),
            pltpu.VMEM((variables, variables, radii), jnp.float32),
        ],
        compiler_params=pltpu.CompilerParams(vmem_limit_bytes=VMEM_LIMIT),
        cost_estimate=pl.CostEstimate(
            flops=state.size * 60, bytes_accessed=state.size * 10, transcendentals=0
        ),
        name="outer",
    )(diffusion, state, below, above, block_inverse, coupling)


def inner_kernel(
    diffusion_ref, table_ref, modes_ref, below_ref, above_ref, inverse_ref, coupling_ref,
    outer_ref, out_ref, own_ref, planes_ref, spread_ref, couple_ref, result_ref, sem,
):
    variables, planes, angles, _ = outer_ref.shape
    first_angle = pl.multiple_of(lax.axis_index("az") * angles, angles)
    own = pltpu.make_async_copy(table_ref.at[pl.ds(first_angle, angles)], own_ref, sem)
    own.start()
    planes_ref[0:PLANE] = below_ref[...]
    planes_ref[PLANE : PLANE * (planes + 1)] = modes_ref[...]
    planes_ref[PLANE * (planes + 1) :] = above_ref[...]
    result_ref[...] = jnp.zeros_like(result_ref)
    for r in range(REACH):
        for u in range(variables):
            spread_ref[r, u] = jnp.broadcast_to(
                inverse_ref[u, :, r : r + 1], (variables, COLUMNS)
            )
        couple_ref[r : r + 1] = jnp.broadcast_to(coupling_ref[:, r : r + 1], (1, COLUMNS))

    shape = (planes, COLUMNS)
    order = lax.broadcasted_iota(jnp.int32, shape, 1) % MODES
    parity = jnp.where(order % 2 == 0, 1.0, -1.0).astype(jnp.float32)
    kept = [order < (k + 1) * MODE_STEP for k in range(CYCLES)]

    def rows(plane, v, r):
        return pl.ds(plane * PLANE + v * SLOT + r, planes, stride=PLANE)

    def mixed(r, source):
        return [
            sum(spread_ref[r, u, v : v + 1, :] * source[v] for v in range(variables))
            for u in range(variables)
        ]

    def filtered(r, values):
        if r >= CYCLES:
            return values
        return [jnp.where(kept[r], value, 0.0) for value in values]

    forcing = []
    for r in range(REACH):
        forcing.append([])
        for v in range(variables):
            here = planes_ref[rows(1, v, r), :]
            below = planes_ref[rows(0, v, r), :]
            above = planes_ref[rows(2, v, r), :]
            forcing[r].append(here + diffusion_ref[v] * (above - 2.0 * here + below))

    solution = [filtered(r, mixed(r, forcing[r])) for r in range(REACH)]
    rims = [solution[CYCLES - 1]]
    for sweep in range(1, ITERS):
        updated = []
        for r in range(REACH - sweep):
            left = solution[r - 1] if r else [parity * value for value in solution[0]]
            right = solution[r + 1]
            couple = couple_ref[r : r + 1]
            source = [
                f + couple * (a + b) for f, a, b in zip(forcing[r], left, right)
            ]
            updated.append(filtered(r, mixed(r, source)))
        solution = updated
        rims.append(solution[CYCLES - 1])

    added = [[None] * (ITERS - 1) for _ in range(ITERS)]
    for sweep in range(1, ITERS):
        for at in range(sweep):
            left = rims[sweep - 1] if at == 0 else added[sweep - 1][at - 1]
            right = added[sweep - 1][at + 1] if at + 1 < ITERS - 1 else None
            if left is None:
                left = right
            elif right is not None:
                left = [a + b for a, b in zip(left, right)]
            if left is None:
                continue
            r = CYCLES + at
            couple = couple_ref[r : r + 1]
            added[sweep][at] = mixed(r, [couple * value for value in left])

    final = solution[:CYCLES] + added[ITERS - 1]
    for r in range(REACH):
        for v in range(variables):
            result_ref[rows(0, v, r), :] = final[r][v]

    own.wait()
    smooth = lax.dot_general(
        own_ref[...], result_ref[...], (((1,), (1,)), ((), ())),
        precision=HIGHEST, preferred_element_type=jnp.float32,
    )
    lane = lax.broadcasted_iota(jnp.int32, (angles, 128), 1)
    for z in range(planes):
        for v in range(variables):
            shift = (z % 2) * PLANE + v * SLOT
            block = smooth[:, (z // 2) * 128 : (z // 2) * 128 + 128]
            block = pltpu.roll(block, 128 - shift, 1) if shift else block
            out_ref[v, z] = outer_ref[v, z] + jnp.where(lane < REACH, block, 0.0)


def inner(table, modes, below, above, block_inverse, coupling, diffusion, outside):
    variables, planes, angles, _ = outside.shape
    at = lambda *index: lambda i: index
    block = (variables, planes, angles, 128)
    return pl.pallas_call(
        inner_kernel,
        grid=(1,),
        out_shape=jax.ShapeDtypeStruct(outside.shape, jnp.float32),
        in_specs=[
            pl.BlockSpec(memory_space=pltpu.SMEM),
            pl.BlockSpec(memory_space=pl.ANY),
            pl.BlockSpec(modes.shape, at(0, 0)),
            pl.BlockSpec(below.shape, at(0, 0)),
            pl.BlockSpec(above.shape, at(0, 0)),
            pl.BlockSpec((variables, variables, 128), at(0, 0, 0)),
            pl.BlockSpec((1, 128), at(0, 0)),
            pl.BlockSpec(block, at(0, 0, 0, 0)),
        ],
        out_specs=pl.BlockSpec(block, at(0, 0, 0, 0)),
        scratch_shapes=[
            pltpu.VMEM((angles, COLUMNS), jnp.float32),
            pltpu.VMEM((PLANE * (planes + 2), COLUMNS), jnp.float32),
            pltpu.VMEM((REACH, variables, variables, COLUMNS), jnp.float32),
            pltpu.VMEM((16, COLUMNS), jnp.float32),
            pltpu.VMEM((PLANE * planes, COLUMNS), jnp.float32),
            pltpu.SemaphoreType.DMA,
        ],
        input_output_aliases={7: 0},
        compiler_params=pltpu.CompilerParams(vmem_limit_bytes=VMEM_LIMIT),
        name="inner",
    )(diffusion, table, modes, below, above, block_inverse, coupling, outside)


def neighbours(first, last):
    count = lax.axis_size("ax")
    forward = [(i, i + 1) for i in range(count - 1)]
    backward = [(target, source) for source, target in forward]
    return lax.ppermute(last, "ax", forward), lax.ppermute(first, "ax", backward)


def body(table, weighted, state, block_inverse, coupling, diffusion):
    coupling = coupling.reshape(1, -1)
    packed, first, last = pack(state, lax.axis_size("az"))
    below, above = neighbours(first, last)
    gathered = lax.all_to_all(packed, "az", 0, 0, tiled=True)
    modes, first, last = transform(weighted, gathered)
    below, above, modes, first, last = lax.optimization_barrier(
        (below, above, modes, first, last)
    )
    modes_below, modes_above = neighbours(first, last)
    outside = outer(state, below, above, block_inverse, coupling, diffusion)
    return inner(
        table, modes, modes_below, modes_above, block_inverse, coupling, diffusion, outside
    )


def solution(mesh):
    def program(state, block_inverse, coupling, diffusion):
        table, weighted = fourier_tables(state.shape[2])
        step = jax.shard_map(
            body,
            mesh=mesh,
            in_specs=(P(), P(), P(None, "ax", "az", None), P(), P(), P()),
            out_specs=P(None, "ax", "az", None),
            check_vma=False,
        )
        return step(
            jnp.asarray(table), jnp.asarray(weighted), state, block_inverse, coupling, diffusion
        )

    return program
```

```python
import jax
import jax.numpy as jnp
import numpy as np
from jax import lax
from jax.experimental import pallas as pl
from jax.experimental.pallas import tpu as pltpu
from jax.sharding import PartitionSpec as P

CYCLES = 8
MODE_STEP = 8
MODES = CYCLES * MODE_STEP
COLUMNS = 2 * MODES
ITERS = 4
REACH = CYCLES + ITERS - 1
SOURCES = 8
SLOT = 12
PLANE = 64
HIGHEST = lax.Precision.HIGHEST
VMEM_LIMIT = 24 * 1024 * 1024
SMALL_LIMIT = 8 * 1024 * 1024
OUTER_WEIGHT = 6000000


def fourier_tables(period):
    angles = np.arange(period)[:, None]
    orders = np.arange(MODES)[None, :]
    phase = (angles * orders % period) * (2.0 * np.pi / period)
    table = np.concatenate([np.cos(phase), np.sin(phase)], axis=1)
    weights = np.where(np.arange(MODES) == 0, 1.0 / period, 2.0 / period)
    weights = np.concatenate([weights, weights])
    return table.astype(np.float32), (table * weights).T.astype(np.float32)


def ring_position():
    at = lax.axis_index("ax")
    return at, at % 2 == 0, lax.axis_size("ax") - 1


def sides(faced, crossed):
    at, even, last = ring_position()
    below = jnp.where(at > 0, jnp.where(even, crossed, faced), 0.0)
    above = jnp.where(at < last, jnp.where(even, faced, crossed), 0.0)
    return below, above


def pack_kernel(state_ref, packed_ref, face_ref, back_ref, inner_ref, sems):
    variables, planes = inner_ref.shape[:2]
    _, even, _ = ring_position()
    facing = jnp.where(even, planes - 1, 0)
    inner = pltpu.make_async_copy(state_ref.at[:, :, :, pl.ds(0, 128)], inner_ref, sems.at[0])
    face = pltpu.make_async_copy(state_ref.at[:, pl.ds(facing, 1)], face_ref, sems.at[1])
    back = pltpu.make_async_copy(
        state_ref.at[:, pl.ds(planes - 1 - facing, 1)], back_ref, sems.at[2]
    )
    inner.start()
    back.start()
    face.start()
    lane = lax.broadcasted_iota(jnp.int32, inner_ref.shape[2:], 1)
    inner.wait()
    for pair in range(planes // 2):
        total = jnp.zeros(inner_ref.shape[2:], jnp.float32)
        for part in range(2):
            for v in range(variables):
                block = jnp.where(lane < REACH, inner_ref[v, 2 * pair + part], 0.0)
                shift = part * PLANE + v * SLOT
                total = total + (pltpu.roll(block, shift, 1) if shift else block)
        for target in range(packed_ref.shape[0]):
            packed_ref[target, :, pair * 128 : pair * 128 + 128] = total
    back.wait()
    face.wait()


def pack(state, devices):
    variables, planes, angles, radii = state.shape
    edge = jax.ShapeDtypeStruct((variables, 1, angles, radii), jnp.float32)
    block = pl.BlockSpec(memory_space=pltpu.VMEM)
    return pl.pallas_call(
        pack_kernel,
        out_shape=[
            jax.ShapeDtypeStruct((devices, angles, planes * PLANE), jnp.float32),
            edge,
            edge,
        ],
        in_specs=[pl.BlockSpec(memory_space=pltpu.HBM)],
        out_specs=[block, block, block],
        scratch_shapes=[
            pltpu.VMEM((variables, planes, angles, 128), jnp.float32),
            pltpu.SemaphoreType.DMA((3,)),
        ],
        compiler_params=pltpu.CompilerParams(vmem_limit_bytes=SMALL_LIMIT),
        name="pack",
    )(state)


def swapped(face, back):
    count = lax.axis_size("ax")
    pairs = [(i, i ^ 1) for i in range(count)]
    across = [(i, (i + (1 if i % 2 else -1)) % count) for i in range(count)]
    crossed = lax.ppermute(back, "ax", across)
    return lax.ppermute(face, "ax", pairs), crossed


def outer_kernel(
    diffusion_ref, table_ref, state_ref, faced_ref, crossed_ref, inverse_ref, coupling_ref,
    out_ref, front_ref, spread_ref, couple_ref, own_ref, start_ref, step_ref, sem,
):
    variables, planes, _, radii = state_ref.shape
    angles = own_ref.shape[0]
    first_angle = pl.multiple_of(lax.axis_index("az") * angles, angles)
    own = pltpu.make_async_copy(table_ref.at[pl.ds(first_angle, angles)], own_ref, sem)

    @pl.when(pl.program_id(0) == 0)
    def _():
        own.start()
        radius = lax.broadcasted_iota(jnp.int32, (variables, radii), 1)
        for u in range(variables):
            rows = jnp.where(radius < CYCLES, 0.0, inverse_ref[u])
            start_ref[u] = rows
            step_ref[u] = rows * coupling_ref[...]
            for r in range(REACH):
                spread_ref[r, u] = jnp.broadcast_to(
                    inverse_ref[u, :, r : r + 1], (variables, COLUMNS)
                )
        for r in range(REACH):
            couple_ref[r : r + 1] = jnp.broadcast_to(coupling_ref[:, r : r + 1], (1, COLUMNS))
        own.wait()

    def mixed(ref, source):
        return [
            sum(ref[u, v : v + 1, :] * source[v] for v in range(variables))
            for u in range(variables)
        ]

    for z in range(planes):
        forcing = []
        for v in range(variables):
            below_end, above_end = sides(faced_ref[v, 0], crossed_ref[v, 0])
            here = state_ref[v, z]
            below = below_end if z == 0 else state_ref[v, z - 1]
            above = above_end if z == planes - 1 else state_ref[v, z + 1]
            forcing.append(here + diffusion_ref[v] * (above - 2.0 * here + below))
        first = mixed(start_ref, forcing)
        solution = first
        for _ in range(ITERS - 1):
            pair = [pltpu.roll(s, 1, 1) + pltpu.roll(s, radii - 1, 1) for s in solution]
            solution = [a + b for a, b in zip(first, mixed(step_ref, pair))]
        for v in range(variables):
            out_ref[v, z] = solution[v]
            front_ref[v, z] = solution[v][:, :128]


def outer(table, state, faced, crossed, block_inverse, coupling, diffusion):
    variables, planes, angles, radii = state.shape
    block = 8
    along = lambda i: (0, 0, i, 0)
    fixed = lambda *index: lambda i: index
    return pl.pallas_call(
        outer_kernel,
        grid=(angles // block,),
        out_shape=[
            jax.ShapeDtypeStruct(state.shape, jnp.float32),
            jax.ShapeDtypeStruct((variables, planes, angles, 128), jnp.float32),
            jax.ShapeDtypeStruct((REACH, variables, variables, COLUMNS), jnp.float32),
            jax.ShapeDtypeStruct((16, COLUMNS), jnp.float32),
            jax.ShapeDtypeStruct((angles, COLUMNS), jnp.float32),
        ],
        in_specs=[
            pl.BlockSpec(memory_space=pltpu.SMEM),
            pl.BlockSpec(memory_space=pl.ANY),
            pl.BlockSpec((variables, planes, block, radii), along),
            pl.BlockSpec((variables, 1, block, radii), along),
            pl.BlockSpec((variables, 1, block, radii), along),
            pl.BlockSpec((variables, variables, radii), fixed(0, 0, 0)),
            pl.BlockSpec((1, radii), fixed(0, 0)),
        ],
        out_specs=[
            pl.BlockSpec((variables, planes, block, radii), along),
            pl.BlockSpec((variables, planes, block, 128), along),
            pl.BlockSpec((REACH, variables, variables, COLUMNS), fixed(0, 0, 0, 0)),
            pl.BlockSpec((16, COLUMNS), fixed(0, 0)),
            pl.BlockSpec((angles, COLUMNS), fixed(0, 0)),
        ],
        scratch_shapes=[
            pltpu.VMEM((variables, variables, radii), jnp.float32),
            pltpu.VMEM((variables, variables, radii), jnp.float32),
            pltpu.SemaphoreType.DMA,
        ],
        compiler_params=pltpu.CompilerParams(vmem_limit_bytes=VMEM_LIMIT),
        cost_estimate=pl.CostEstimate(
            flops=state.size * OUTER_WEIGHT, bytes_accessed=state.size * 10, transcendentals=0
        ),
        name="outer",
    )(diffusion, table, state, faced, crossed, block_inverse, coupling)


def solve_kernel(
    diffusion_ref, weighted_ref, gathered_ref, spread_ref, couple_ref, own_ref,
    smooth_ref, beyond_ref, forcing_ref, result_ref,
):
    variables = diffusion_ref.shape[0]
    planes = gathered_ref.shape[2] // PLANE
    modes = jnp.dot(
        weighted_ref[...], gathered_ref[...].reshape(-1, PLANE * planes),
        precision=HIGHEST, preferred_element_type=jnp.float32,
    ).T
    plane = [modes[z * PLANE : (z + 1) * PLANE] for z in range(planes)]
    slot = lax.broadcasted_iota(jnp.int32, (PLANE, COLUMNS), 0) // SLOT
    rates = jnp.zeros((PLANE, COLUMNS), jnp.float32)
    for v in range(variables):
        rates = jnp.where(slot == v, diffusion_ref[v], rates)
    for z in range(planes):
        around = [plane[n] for n in (z - 1, z + 1) if 0 <= n < planes]
        forcing_ref[z * PLANE : (z + 1) * PLANE] = plane[z] + rates * (
            sum(around) - 2.0 * plane[z]
        )
    forcing_ref[planes * PLANE : (planes + 1) * PLANE] = rates * plane[0]
    forcing_ref[(planes + 1) * PLANE : (planes + 2) * PLANE] = rates * plane[planes - 1]
    forcing_ref[(planes + 2) * PLANE :] = jnp.zeros(
        (forcing_ref.shape[0] - (planes + 2) * PLANE, COLUMNS), jnp.float32
    )
    result_ref[...] = jnp.zeros_like(result_ref)

    shape = (SOURCES, COLUMNS)
    order = lax.broadcasted_iota(jnp.int32, shape, 1) % MODES
    parity = jnp.where(order % 2 == 0, 1.0, -1.0).astype(jnp.float32)
    kept = [order < (k + 1) * MODE_STEP for k in range(CYCLES)]

    def rows(v, r):
        return pl.ds(v * SLOT + r, SOURCES, stride=PLANE)

    def mixed(r, source):
        return [
            sum(spread_ref[r, u, v : v + 1, :] * source[v] for v in range(variables))
            for u in range(variables)
        ]

    def filtered(r, values):
        if r >= CYCLES:
            return values
        return [jnp.where(kept[r], value, 0.0) for value in values]

    forcing = [[forcing_ref[rows(v, r), :] for v in range(variables)] for r in range(REACH)]
    solution = [filtered(r, mixed(r, forcing[r])) for r in range(REACH)]
    rims = [solution[CYCLES - 1]]
    for sweep in range(1, ITERS):
        updated = []
        for r in range(REACH - sweep):
            left = solution[r - 1] if r else [parity * value for value in solution[0]]
            right = solution[r + 1]
            couple = couple_ref[r : r + 1]
            source = [
                f + couple * (a + b) for f, a, b in zip(forcing[r], left, right)
            ]
            updated.append(filtered(r, mixed(r, source)))
        solution = updated
        rims.append(solution[CYCLES - 1])

    added = [[None] * (ITERS - 1) for _ in range(ITERS)]
    for sweep in range(1, ITERS):
        for at in range(sweep):
            left = rims[sweep - 1] if at == 0 else added[sweep - 1][at - 1]
            right = added[sweep - 1][at + 1] if at + 1 < ITERS - 1 else None
            if left is None:
                left = right
            elif right is not None:
                left = [a + b for a, b in zip(left, right)]
            if left is None:
                continue
            r = CYCLES + at
            couple = couple_ref[r : r + 1]
            added[sweep][at] = mixed(r, [couple * value for value in left])

    final = solution[:CYCLES] + added[ITERS - 1]
    for r in range(REACH):
        for v in range(variables):
            result_ref[rows(v, r), :] = final[r][v]

    smooth = lax.dot_general(
        own_ref[...], result_ref[0 : (planes + 2) * PLANE, :], (((1,), (1,)), ((), ())),
        precision=HIGHEST, preferred_element_type=jnp.float32,
    )
    smooth_ref[...] = smooth[:, : planes * PLANE]
    beyond_ref[...] = smooth[:, planes * PLANE :]


def solve(diffusion, weighted, gathered, spread, couple, own):
    angles = own.shape[0]
    block = pl.BlockSpec(memory_space=pltpu.VMEM)
    return pl.pallas_call(
        solve_kernel,
        out_shape=[
            jax.ShapeDtypeStruct((angles, gathered.shape[2]), jnp.float32),
            jax.ShapeDtypeStruct((angles, 2 * PLANE), jnp.float32),
        ],
        in_specs=[pl.BlockSpec(memory_space=pltpu.SMEM)] + [block] * 5,
        out_specs=[block, block],
        scratch_shapes=[
            pltpu.VMEM((PLANE * SOURCES, COLUMNS), jnp.float32),
            pltpu.VMEM((PLANE * SOURCES, COLUMNS), jnp.float32),
        ],
        compiler_params=pltpu.CompilerParams(vmem_limit_bytes=SMALL_LIMIT),
        name="solve",
    )(diffusion, weighted, gathered, spread, couple, own)


def placed(smooth, start):
    tile = smooth[:, start // 128 * 128 : start // 128 * 128 + 128]
    tile = pltpu.roll(tile, 128 - start % 128, 1) if start % 128 else tile
    return jnp.where(lax.broadcasted_iota(jnp.int32, tile.shape, 1) < REACH, tile, 0.0)


def middle_kernel(smooth_ref, front_ref, outer_ref, out_ref, ends_ref, block_ref, sem):
    del outer_ref
    variables, planes, _, lanes = front_ref.shape
    for z in (*range(1, planes - 1), 0, planes - 1):
        for v in range(variables):
            tile = front_ref[v, z] + placed(smooth_ref[...], z * PLANE + v * SLOT)
            if z in (0, planes - 1):
                ends_ref[v, min(z, 1)] = tile
            else:
                block_ref[v, z - 1] = tile
        if z == planes - 2:
            copy = pltpu.make_async_copy(
                block_ref, out_ref.at[:, pl.ds(1, planes - 2), :, pl.ds(0, lanes)], sem
            )
            copy.start()
    copy.wait()


def middle(smooth, front, outside):
    variables, planes, angles, lanes = front.shape
    block = pl.BlockSpec(memory_space=pltpu.VMEM)
    whole = pl.BlockSpec(memory_space=pltpu.HBM)
    return pl.pallas_call(
        middle_kernel,
        out_shape=[
            jax.ShapeDtypeStruct(outside.shape, jnp.float32),
            jax.ShapeDtypeStruct((variables, 2, angles, lanes), jnp.float32),
        ],
        in_specs=[block, block, whole],
        out_specs=[whole, block],
        scratch_shapes=[
            pltpu.VMEM((variables, planes - 2, angles, lanes), jnp.float32),
            pltpu.SemaphoreType.DMA,
        ],
        input_output_aliases={2: 0},
        compiler_params=pltpu.CompilerParams(vmem_limit_bytes=SMALL_LIMIT),
        name="middle",
    )(smooth, front, outside)


def ends_kernel(faced_ref, crossed_ref, ends_ref, middle_ref, out_ref, block_ref, sems):
    del middle_ref
    variables, _, _, lanes = ends_ref.shape
    below, above = sides(faced_ref[...], crossed_ref[...])
    copies = []
    for at, (tile, start, z) in enumerate(
        ((below, PLANE, 0), (above, 0, out_ref.shape[1] - 1))
    ):
        for v in range(variables):
            block_ref[at, v, 0] = ends_ref[v, at] + placed(tile, start + v * SLOT)
        copies.append(
            pltpu.make_async_copy(
                block_ref.at[at], out_ref.at[:, pl.ds(z, 1), :, pl.ds(0, lanes)], sems.at[at]
            )
        )
        copies[at].start()
    for copy in copies:
        copy.wait()


def ends(faced, crossed, edges, outside):
    variables, _, angles, lanes = edges.shape
    block = pl.BlockSpec(memory_space=pltpu.VMEM)
    whole = pl.BlockSpec(memory_space=pltpu.HBM)
    return pl.pallas_call(
        ends_kernel,
        out_shape=jax.ShapeDtypeStruct(outside.shape, jnp.float32),
        in_specs=[block, block, block, whole],
        out_specs=whole,
        scratch_shapes=[
            pltpu.VMEM((2, variables, 1, angles, lanes), jnp.float32),
            pltpu.SemaphoreType.DMA((2,)),
        ],
        input_output_aliases={3: 0},
        compiler_params=pltpu.CompilerParams(vmem_limit_bytes=SMALL_LIMIT),
        name="ends",
    )(faced, crossed, edges, outside)


def body(table, weighted, state, block_inverse, coupling, diffusion):
    coupling = coupling.reshape(1, -1)
    packed, face, back = pack(state, lax.axis_size("az"))
    faced, crossed = swapped(face, back)
    gathered = lax.all_to_all(packed, "az", 0, 0, tiled=True)
    outside, front, spread, couple, own = outer(
        table, state, faced, crossed, block_inverse, coupling, diffusion
    )
    gathered, outside, front, spread, couple, own = lax.optimization_barrier(
        (gathered, outside, front, spread, couple, own)
    )
    smooth, beyond = solve(diffusion, weighted, gathered, spread, couple, own)
    faced, crossed = swapped(beyond, beyond)
    outside, edges = middle(smooth, front, outside)
    return ends(faced, crossed, edges, outside)


def solution(mesh):
    def program(state, block_inverse, coupling, diffusion):
        table, weighted = fourier_tables(state.shape[2])
        step = jax.shard_map(
            body,
            mesh=mesh,
            in_specs=(P(), P(), P(None, "ax", "az", None), P(), P(), P()),
            out_specs=P(None, "ax", "az", None),
            check_vma=False,
        )
        return step(
            jnp.asarray(table), jnp.asarray(weighted), state, block_inverse, coupling, diffusion
        )

    return program
```

```python
import jax
import jax.numpy as jnp
import numpy as np
from jax import lax
from jax.experimental import pallas as pl
from jax.experimental.pallas import tpu as pltpu
from jax.sharding import PartitionSpec as P

CYCLES = 8
MODE_STEP = 8
MODES = CYCLES * MODE_STEP
COLUMNS = 2 * MODES
ITERS = 4
REACH = CYCLES + ITERS - 1
SOURCES = 8
SLOT = 12
PLANE = 64
HIGHEST = lax.Precision.HIGHEST
VMEM_LIMIT = 12 * 1024 * 1024
SMALL_LIMIT = 8 * 1024 * 1024
OUTER_WEIGHT = 6000000


def fourier_tables(period):
    angles = np.arange(period)[:, None]
    orders = np.arange(MODES)[None, :]
    phase = (angles * orders % period) * (2.0 * np.pi / period)
    table = np.concatenate([np.cos(phase), np.sin(phase)], axis=1)
    weights = np.where(np.arange(MODES) == 0, 1.0 / period, 2.0 / period)
    weights = np.concatenate([weights, weights])
    return table.astype(np.float32), (table * weights).T.astype(np.float32)


def ring_position():
    at = lax.axis_index("ax")
    return at, at % 2 == 0, lax.axis_size("ax") - 1


def sides(faced, crossed):
    at, even, last = ring_position()
    below = jnp.where(at > 0, jnp.where(even, crossed, faced), 0.0)
    above = jnp.where(at < last, jnp.where(even, faced, crossed), 0.0)
    return below, above


def pack_kernel(state_ref, packed_ref, face_ref, back_ref, inner_ref, sems):
    variables, planes = inner_ref.shape[:2]
    _, even, _ = ring_position()
    facing = jnp.where(even, planes - 1, 0)
    inner = pltpu.make_async_copy(state_ref.at[:, :, :, pl.ds(0, 128)], inner_ref, sems.at[0])
    face = pltpu.make_async_copy(state_ref.at[:, pl.ds(facing, 1)], face_ref, sems.at[1])
    back = pltpu.make_async_copy(
        state_ref.at[:, pl.ds(planes - 1 - facing, 1)], back_ref, sems.at[2]
    )
    inner.start()
    back.start()
    face.start()
    lane = lax.broadcasted_iota(jnp.int32, inner_ref.shape[2:], 1)
    inner.wait()
    for pair in range(planes // 2):
        total = jnp.zeros(inner_ref.shape[2:], jnp.float32)
        for part in range(2):
            for v in range(variables):
                block = jnp.where(lane < REACH, inner_ref[v, 2 * pair + part], 0.0)
                shift = part * PLANE + v * SLOT
                total = total + (pltpu.roll(block, shift, 1) if shift else block)
        for target in range(packed_ref.shape[0]):
            packed_ref[target, :, pair * 128 : pair * 128 + 128] = total
    back.wait()
    face.wait()


def pack(state, devices):
    variables, planes, angles, radii = state.shape
    edge = jax.ShapeDtypeStruct((variables, 1, angles, radii), jnp.float32)
    block = pl.BlockSpec(memory_space=pltpu.VMEM)
    return pl.pallas_call(
        pack_kernel,
        out_shape=[
            jax.ShapeDtypeStruct((devices, angles, planes * PLANE), jnp.float32),
            edge,
            edge,
        ],
        in_specs=[pl.BlockSpec(memory_space=pltpu.HBM)],
        out_specs=[block, block, block],
        scratch_shapes=[
            pltpu.VMEM((variables, planes, angles, 128), jnp.float32),
            pltpu.SemaphoreType.DMA((3,)),
        ],
        compiler_params=pltpu.CompilerParams(vmem_limit_bytes=SMALL_LIMIT),
        name="pack",
    )(state)


def swapped(face, back):
    count = lax.axis_size("ax")
    pairs = [(i, i ^ 1) for i in range(count)]
    across = []
    for i in range(lax.axis_size("az")):
        for j in range(count):
            to = j + 1 if j % 2 else j - 1
            target = (i, to) if 0 <= to < count else (i ^ 1, j)
            across.append((i * count + j, target[0] * count + target[1]))
    crossed = lax.ppermute(back, ("az", "ax"), across)
    return lax.ppermute(face, "ax", pairs), crossed


def outer_kernel(
    diffusion_ref, table_ref, state_ref, faced_ref, crossed_ref, inverse_ref, coupling_ref,
    out_ref, front_ref, spread_ref, couple_ref, own_ref,
    start_ref, step_ref, first_ref, turn_ref, done_ref, own_sem, out_sems,
):
    variables, planes, angles, radii = state_ref.shape
    first_angle = pl.multiple_of(lax.axis_index("az") * angles, angles)
    own = pltpu.make_async_copy(
        table_ref.at[pl.ds(first_angle, angles)], own_ref, own_sem
    )
    own.start()
    radius = lax.broadcasted_iota(jnp.int32, (variables, radii), 1)
    for u in range(variables):
        rows = jnp.where(radius < CYCLES, 0.0, inverse_ref[u])
        start_ref[u] = rows
        step_ref[u] = rows * coupling_ref[...]
        for r in range(REACH):
            spread_ref[r, u] = jnp.broadcast_to(
                inverse_ref[u, :, r : r + 1], (variables, COLUMNS)
            )
    for r in range(REACH):
        couple_ref[r : r + 1] = jnp.broadcast_to(coupling_ref[:, r : r + 1], (1, COLUMNS))

    tiles = [slice(at, at + 128) for at in range(0, radii, 128)]
    lane = lax.broadcasted_iota(jnp.int32, (angles, 128), 1)

    def mixed(ref, u, cut, source):
        return sum(ref[u, v : v + 1, cut] * source[v] for v in range(variables))

    def turned(source, cut, by):
        return [pltpu.roll(source[v, :, cut], by % 128, 1) for v in range(variables)]

    stores = []
    for z in (*range(1, planes - 1), 0, planes - 1):
        result = done_ref.at[z]
        for cut in tiles:
            forcing = []
            for v in range(variables):
                here = state_ref[v, z, :, cut]
                below, above = sides(faced_ref[v, 0, :, cut], crossed_ref[v, 0, :, cut])
                if z > 0:
                    below = state_ref[v, z - 1, :, cut]
                if z < planes - 1:
                    above = state_ref[v, z + 1, :, cut]
                forcing.append(here + diffusion_ref[v] * (above - 2.0 * here + below))
            for u in range(variables):
                first_ref[u, :, cut] = mixed(start_ref, u, cut, forcing)
        for sweep in range(1, ITERS):
            source = first_ref if sweep == 1 else turn_ref.at[sweep % 2]
            target = result if sweep == ITERS - 1 else turn_ref.at[(sweep + 1) % 2]
            before = None
            ahead = turned(source, tiles[0], -1)
            for at, cut in enumerate(tiles):
                inward = turned(source, cut, 1)
                left = inward if before is None else [
                    jnp.where(lane == 0, a, b) for a, b in zip(before, inward)
                ]
                outward = ahead
                if at + 1 < len(tiles):
                    ahead = turned(source, tiles[at + 1], -1)
                else:
                    ahead = [jnp.zeros((angles, 128), jnp.float32)] * variables
                right = [jnp.where(lane == 127, a, b) for a, b in zip(ahead, outward)]
                pair = [a + b for a, b in zip(left, right)]
                for u in range(variables):
                    target[u, :, cut] = first_ref[u, :, cut] + mixed(step_ref, u, cut, pair)
                before = inward
        for v in range(variables):
            front_ref[v, z] = result[v, :, tiles[0]]
        store = pltpu.make_async_copy(done_ref.at[z], out_ref.at[:, z], out_sems.at[z])
        store.start()
        stores.append(store)
    own.wait()
    for store in stores:
        store.wait()


def outer(table, state, faced, crossed, block_inverse, coupling, diffusion):
    variables, planes, angles, radii = state.shape
    block = pl.BlockSpec(memory_space=pltpu.VMEM)
    whole = pl.BlockSpec(memory_space=pl.ANY)
    rows = (variables, variables, radii)
    return pl.pallas_call(
        outer_kernel,
        out_shape=[
            jax.ShapeDtypeStruct(state.shape, jnp.float32),
            jax.ShapeDtypeStruct((variables, planes, angles, 128), jnp.float32),
            jax.ShapeDtypeStruct((REACH, variables, variables, COLUMNS), jnp.float32),
            jax.ShapeDtypeStruct((16, COLUMNS), jnp.float32),
            jax.ShapeDtypeStruct((angles, COLUMNS), jnp.float32),
        ],
        in_specs=[
            pl.BlockSpec(memory_space=pltpu.SMEM), whole, block, block, block, block, block,
        ],
        out_specs=[whole, block, block, block, block],
        scratch_shapes=[
            pltpu.VMEM(rows, jnp.float32),
            pltpu.VMEM(rows, jnp.float32),
            pltpu.VMEM((variables, angles, radii), jnp.float32),
            pltpu.VMEM((2, variables, angles, radii), jnp.float32),
            pltpu.VMEM((planes, variables, angles, radii), jnp.float32),
            pltpu.SemaphoreType.DMA,
            pltpu.SemaphoreType.DMA((planes,)),
        ],
        compiler_params=pltpu.CompilerParams(vmem_limit_bytes=VMEM_LIMIT),
        cost_estimate=pl.CostEstimate(
            flops=state.size * OUTER_WEIGHT, bytes_accessed=state.size * 10, transcendentals=0
        ),
        name="outer",
    )(diffusion, table, state, faced, crossed, block_inverse, coupling)


def solve_kernel(
    diffusion_ref, weighted_ref, gathered_ref, spread_ref, couple_ref, own_ref,
    smooth_ref, beyond_ref, forcing_ref, result_ref,
):
    variables = diffusion_ref.shape[0]
    planes = gathered_ref.shape[2] // PLANE
    modes = jnp.dot(
        weighted_ref[...], gathered_ref[...].reshape(-1, PLANE * planes),
        precision=HIGHEST, preferred_element_type=jnp.float32,
    ).T
    plane = [modes[z * PLANE : (z + 1) * PLANE] for z in range(planes)]
    slot = lax.broadcasted_iota(jnp.int32, (PLANE, COLUMNS), 0) // SLOT
    rates = jnp.zeros((PLANE, COLUMNS), jnp.float32)
    for v in range(variables):
        rates = jnp.where(slot == v, diffusion_ref[v], rates)
    for z in range(planes):
        around = [plane[n] for n in (z - 1, z + 1) if 0 <= n < planes]
        forcing_ref[z * PLANE : (z + 1) * PLANE] = plane[z] + rates * (
            sum(around) - 2.0 * plane[z]
        )
    forcing_ref[planes * PLANE : (planes + 1) * PLANE] = rates * plane[0]
    forcing_ref[(planes + 1) * PLANE : (planes + 2) * PLANE] = rates * plane[planes - 1]
    forcing_ref[(planes + 2) * PLANE :] = jnp.zeros(
        (forcing_ref.shape[0] - (planes + 2) * PLANE, COLUMNS), jnp.float32
    )
    result_ref[...] = jnp.zeros_like(result_ref)

    shape = (SOURCES, COLUMNS)
    order = lax.broadcasted_iota(jnp.int32, shape, 1) % MODES
    parity = jnp.where(order % 2 == 0, 1.0, -1.0).astype(jnp.float32)
    kept = [order < (k + 1) * MODE_STEP for k in range(CYCLES)]

    def rows(v, r):
        return pl.ds(v * SLOT + r, SOURCES, stride=PLANE)

    def mixed(r, source):
        return [
            sum(spread_ref[r, u, v : v + 1, :] * source[v] for v in range(variables))
            for u in range(variables)
        ]

    def filtered(r, values):
        if r >= CYCLES:
            return values
        return [jnp.where(kept[r], value, 0.0) for value in values]

    forcing = [[forcing_ref[rows(v, r), :] for v in range(variables)] for r in range(REACH)]
    solution = [filtered(r, mixed(r, forcing[r])) for r in range(REACH)]
    rims = [solution[CYCLES - 1]]
    for sweep in range(1, ITERS):
        updated = []
        for r in range(REACH - sweep):
            left = solution[r - 1] if r else [parity * value for value in solution[0]]
            right = solution[r + 1]
            couple = couple_ref[r : r + 1]
            source = [
                f + couple * (a + b) for f, a, b in zip(forcing[r], left, right)
            ]
            updated.append(filtered(r, mixed(r, source)))
        solution = updated
        rims.append(solution[CYCLES - 1])

    added = [[None] * (ITERS - 1) for _ in range(ITERS)]
    for sweep in range(1, ITERS):
        for at in range(sweep):
            left = rims[sweep - 1] if at == 0 else added[sweep - 1][at - 1]
            right = added[sweep - 1][at + 1] if at + 1 < ITERS - 1 else None
            if left is None:
                left = right
            elif right is not None:
                left = [a + b for a, b in zip(left, right)]
            if left is None:
                continue
            r = CYCLES + at
            couple = couple_ref[r : r + 1]
            added[sweep][at] = mixed(r, [couple * value for value in left])

    final = solution[:CYCLES] + added[ITERS - 1]
    for r in range(REACH):
        for v in range(variables):
            result_ref[rows(v, r), :] = final[r][v]

    smooth = lax.dot_general(
        own_ref[...], result_ref[0 : (planes + 2) * PLANE, :], (((1,), (1,)), ((), ())),
        precision=HIGHEST, preferred_element_type=jnp.float32,
    )
    smooth_ref[...] = smooth[:, : planes * PLANE]
    beyond_ref[...] = smooth[:, planes * PLANE :]


def solve(diffusion, weighted, gathered, spread, couple, own):
    angles = own.shape[0]
    block = pl.BlockSpec(memory_space=pltpu.VMEM)
    return pl.pallas_call(
        solve_kernel,
        out_shape=[
            jax.ShapeDtypeStruct((angles, gathered.shape[2]), jnp.float32),
            jax.ShapeDtypeStruct((angles, 2 * PLANE), jnp.float32),
        ],
        in_specs=[pl.BlockSpec(memory_space=pltpu.SMEM)] + [block] * 5,
        out_specs=[block, block],
        scratch_shapes=[
            pltpu.VMEM((PLANE * SOURCES, COLUMNS), jnp.float32),
            pltpu.VMEM((PLANE * SOURCES, COLUMNS), jnp.float32),
        ],
        compiler_params=pltpu.CompilerParams(vmem_limit_bytes=SMALL_LIMIT),
        name="solve",
    )(diffusion, weighted, gathered, spread, couple, own)


def placed(smooth, start):
    tile = smooth[:, start // 128 * 128 : start // 128 * 128 + 128]
    tile = pltpu.roll(tile, 128 - start % 128, 1) if start % 128 else tile
    return jnp.where(lax.broadcasted_iota(jnp.int32, tile.shape, 1) < REACH, tile, 0.0)


def middle_kernel(smooth_ref, front_ref, outer_ref, out_ref, ends_ref, block_ref, sem):
    del outer_ref
    variables, planes, _, lanes = front_ref.shape
    for z in (*range(1, planes - 1), 0, planes - 1):
        for v in range(variables):
            tile = front_ref[v, z] + placed(smooth_ref[...], z * PLANE + v * SLOT)
            if z in (0, planes - 1):
                ends_ref[v, min(z, 1)] = tile
            else:
                block_ref[v, z - 1] = tile
        if z == planes - 2:
            copy = pltpu.make_async_copy(
                block_ref, out_ref.at[:, pl.ds(1, planes - 2), :, pl.ds(0, lanes)], sem
            )
            copy.start()
    copy.wait()


def middle(smooth, front, outside):
    variables, planes, angles, lanes = front.shape
    block = pl.BlockSpec(memory_space=pltpu.VMEM)
    whole = pl.BlockSpec(memory_space=pltpu.HBM)
    return pl.pallas_call(
        middle_kernel,
        out_shape=[
            jax.ShapeDtypeStruct(outside.shape, jnp.float32),
            jax.ShapeDtypeStruct((variables, 2, angles, lanes), jnp.float32),
        ],
        in_specs=[block, block, whole],
        out_specs=[whole, block],
        scratch_shapes=[
            pltpu.VMEM((variables, planes - 2, angles, lanes), jnp.float32),
            pltpu.SemaphoreType.DMA,
        ],
        input_output_aliases={2: 0},
        compiler_params=pltpu.CompilerParams(vmem_limit_bytes=SMALL_LIMIT),
        name="middle",
    )(smooth, front, outside)


def ends_kernel(faced_ref, crossed_ref, ends_ref, middle_ref, out_ref, block_ref, sems):
    del middle_ref
    variables, _, _, lanes = ends_ref.shape
    below, above = sides(faced_ref[...], crossed_ref[...])
    copies = []
    for at, (tile, start, z) in enumerate(
        ((below, PLANE, 0), (above, 0, out_ref.shape[1] - 1))
    ):
        for v in range(variables):
            block_ref[at, v, 0] = ends_ref[v, at] + placed(tile, start + v * SLOT)
        copies.append(
            pltpu.make_async_copy(
                block_ref.at[at], out_ref.at[:, pl.ds(z, 1), :, pl.ds(0, lanes)], sems.at[at]
            )
        )
        copies[at].start()
    for copy in copies:
        copy.wait()


def ends(faced, crossed, edges, outside):
    variables, _, angles, lanes = edges.shape
    block = pl.BlockSpec(memory_space=pltpu.VMEM)
    whole = pl.BlockSpec(memory_space=pltpu.HBM)
    return pl.pallas_call(
        ends_kernel,
        out_shape=jax.ShapeDtypeStruct(outside.shape, jnp.float32),
        in_specs=[block, block, block, whole],
        out_specs=whole,
        scratch_shapes=[
            pltpu.VMEM((2, variables, 1, angles, lanes), jnp.float32),
            pltpu.SemaphoreType.DMA((2,)),
        ],
        input_output_aliases={3: 0},
        compiler_params=pltpu.CompilerParams(vmem_limit_bytes=SMALL_LIMIT),
        name="ends",
    )(faced, crossed, edges, outside)


def body(table, weighted, state, block_inverse, coupling, diffusion):
    coupling = coupling.reshape(1, -1)
    packed, face, back = pack(pltpu.with_memory_space_constraint(state, pltpu.HBM), lax.axis_size("az"))
    faced, crossed = swapped(face, back)
    gathered = lax.all_to_all(packed, "az", 0, 0, tiled=True)
    outside, front, spread, couple, own = outer(
        table, state, faced, crossed, block_inverse, coupling, diffusion
    )
    gathered, outside, front, spread, couple, own = lax.optimization_barrier(
        (gathered, outside, front, spread, couple, own)
    )
    smooth, beyond = solve(diffusion, weighted, gathered, spread, couple, own)
    faced, crossed = swapped(beyond, beyond)
    outside, edges = middle(smooth, front, outside)
    return ends(faced, crossed, edges, outside)


def solution(mesh):
    def program(state, block_inverse, coupling, diffusion):
        table, weighted = fourier_tables(state.shape[2])
        step = jax.shard_map(
            body,
            mesh=mesh,
            in_specs=(P(), P(), P(None, "ax", "az", None), P(), P(), P()),
            out_specs=P(None, "ax", "az", None),
            check_vma=False,
        )
        return step(
            jnp.asarray(table), jnp.asarray(weighted), state, block_inverse, coupling, diffusion
        )

    return program
```

```python
import jax
import jax.numpy as jnp
import ml_dtypes
import numpy as np
from jax import lax
from jax.experimental import pallas as pl
from jax.experimental.pallas import tpu as pltpu
from jax.sharding import PartitionSpec as P

CYCLES = 8
MODE_STEP = 8
MODES = CYCLES * MODE_STEP
COLUMNS = 2 * MODES
ITERS = 4
REACH = CYCLES + ITERS - 1
ORDER = (1, 2, 0, 3)
SLOT = 12
PLANE = 64
VMEM_LIMIT = 12 * 1024 * 1024
SMALL_LIMIT = 8 * 1024 * 1024
CHUNKS_WEIGHT = 20000000000
OUTER_WEIGHT = 60000


def fourier_tables(period):
    angles = np.arange(period)[:, None]
    orders = np.arange(MODES)[None, :]
    phase = (angles * orders % period) * (2.0 * np.pi / period)
    table = np.concatenate([np.cos(phase), np.sin(phase)], axis=1)
    weights = np.where(np.arange(MODES) == 0, 1.0 / period, 2.0 / period)
    weights = np.concatenate([weights, weights])
    weighted = (table * weights).T.astype(np.float32)
    high = weighted.astype(ml_dtypes.bfloat16)
    low = (weighted - high.astype(np.float32)).astype(ml_dtypes.bfloat16)
    return table.astype(np.float32), np.concatenate([high, low], axis=0)


def ring_position():
    at = lax.axis_index("ax")
    return at, at % 2 == 0, lax.axis_size("ax") - 1


def sides(faced, crossed):
    at, even, last = ring_position()
    below = jnp.where(at > 0, jnp.where(even, crossed, faced), 0.0)
    above = jnp.where(at < last, jnp.where(even, faced, crossed), 0.0)
    return below, above


def packed(blocks):
    lane = lax.broadcasted_iota(jnp.int32, blocks[0].shape, 1)
    total = jnp.zeros(blocks[0].shape, jnp.float32)
    for v, block in enumerate(blocks):
        block = jnp.where(lane < REACH, block, 0.0)
        total = total + (pltpu.roll(block, v * SLOT, 1) if v else block)
    return total


def pack_kernel(state_ref, middle_ref, edges_ref, face_ref, back_ref, inner_ref, sems):
    variables, planes = inner_ref.shape[:2]
    _, even, _ = ring_position()
    facing = jnp.where(even, planes - 1, 0)
    inner = pltpu.make_async_copy(state_ref.at[:, :, :, pl.ds(0, 128)], inner_ref, sems.at[0])
    face = pltpu.make_async_copy(state_ref.at[:, pl.ds(facing, 1)], face_ref, sems.at[1])
    back = pltpu.make_async_copy(
        state_ref.at[:, pl.ds(planes - 1 - facing, 1)], back_ref, sems.at[2]
    )
    inner.start()
    face.start()
    back.start()
    inner.wait()
    for target, pair in ((middle_ref, ORDER[:2]), (edges_ref, ORDER[2:])):
        first, second = (packed([inner_ref[v, z] for v in range(variables)]) for z in pair)
        target[...] = first + pltpu.roll(second, PLANE, 1)
    face.wait()
    back.wait()


def pack(state):
    variables, planes, angles, radii = state.shape
    tile = jax.ShapeDtypeStruct((angles, 128), jnp.float32)
    edge = jax.ShapeDtypeStruct((variables, 1, angles, radii), jnp.float32)
    block = pl.BlockSpec(memory_space=pltpu.VMEM)
    return pl.pallas_call(
        pack_kernel,
        out_shape=[tile, tile, edge, edge],
        in_specs=[pl.BlockSpec(memory_space=pl.ANY)],
        out_specs=[block] * 4,
        scratch_shapes=[
            pltpu.VMEM((variables, planes, angles, 128), jnp.float32),
            pltpu.SemaphoreType.DMA((3,)),
        ],
        compiler_params=pltpu.CompilerParams(vmem_limit_bytes=SMALL_LIMIT),
        name="pack",
    )(state)


def chunks_kernel(diffusion_ref, middle_ref, edges_ref, faced_ref, crossed_ref, out_ref):
    middle, edges = middle_ref[...], edges_ref[...]
    lane = lax.broadcasted_iota(jnp.int32, middle.shape, 1)
    slot = lane % PLANE // SLOT
    rates = jnp.zeros(middle.shape, jnp.float32)
    for v in range(diffusion_ref.shape[0]):
        rates = jnp.where(slot == v, diffusion_ref[v], rates)
    faced = packed([faced_ref[v, 0, :, :128] for v in range(faced_ref.shape[0])])
    below, above = sides(
        faced + pltpu.roll(faced, PLANE, 1), pltpu.roll(crossed_ref[...], PLANE, 1)
    )
    beyond = jnp.where(lane < PLANE, below, above)
    around = (edges + pltpu.roll(middle, PLANE, 1), beyond + middle)
    for at, here in enumerate((middle, edges)):
        forcing = here + rates * (around[at] - 2.0 * here)
        for target in range(out_ref.shape[0]):
            out_ref[target, :, at * 128 : at * 128 + 128] = forcing


def forcing_chunks(diffusion, middle, edges, faced, crossed, devices):
    angles, lanes = middle.shape
    block = pl.BlockSpec(memory_space=pltpu.VMEM)
    return pl.pallas_call(
        chunks_kernel,
        out_shape=jax.ShapeDtypeStruct((devices, angles, 2 * lanes), jnp.float32),
        in_specs=[pl.BlockSpec(memory_space=pltpu.SMEM)] + [block] * 4,
        out_specs=block,
        compiler_params=pltpu.CompilerParams(vmem_limit_bytes=SMALL_LIMIT),
        cost_estimate=pl.CostEstimate(
            flops=CHUNKS_WEIGHT, bytes_accessed=devices * angles * lanes * 8, transcendentals=0
        ),
        name="chunks",
    )(diffusion, middle, edges, faced, crossed)


def across_chips(block):
    count = lax.axis_size("ax")
    route = []
    for i in range(lax.axis_size("az")):
        for j in range(count):
            to = j + 1 if j % 2 else j - 1
            target = (i, to) if 0 <= to < count else (i ^ 1, j)
            route.append((i * count + j, target[0] * count + target[1]))
    return lax.ppermute(block, ("az", "ax"), route)


def between_cores(block):
    return lax.ppermute(block, "ax", [(i, i ^ 1) for i in range(lax.axis_size("ax"))])


def outer_kernel(
    diffusion_ref, table_ref, state_ref, faced_ref, crossed_ref, inverse_ref, coupling_ref,
    out_ref, front_ref, spread_ref, couple_ref, own_ref,
    start_ref, step_ref, first_ref, turn_ref, done_ref, own_sem, out_sems,
):
    variables, planes, angles, radii = state_ref.shape
    first_angle = pl.multiple_of(lax.axis_index("az") * angles, angles)
    own = pltpu.make_async_copy(
        table_ref.at[pl.ds(first_angle, angles)], own_ref, own_sem
    )
    own.start()
    radius = lax.broadcasted_iota(jnp.int32, (variables, radii), 1)
    for u in range(variables):
        rows = jnp.where(radius < CYCLES, 0.0, inverse_ref[u])
        start_ref[u] = rows
        step_ref[u] = rows * coupling_ref[...]
        for r in range(REACH):
            spread_ref[r, u] = jnp.broadcast_to(
                inverse_ref[u, :, r : r + 1], (variables, COLUMNS)
            )
    for r in range(REACH):
        couple_ref[r : r + 1] = jnp.broadcast_to(coupling_ref[:, r : r + 1], (1, COLUMNS))

    tiles = [slice(at, at + 128) for at in range(0, radii, 128)]
    lane = lax.broadcasted_iota(jnp.int32, (angles, 128), 1)

    def mixed(ref, u, cut, source):
        return sum(ref[u, v : v + 1, cut] * source[v] for v in range(variables))

    def turned(source, cut, by):
        return [pltpu.roll(source[v, :, cut], by % 128, 1) for v in range(variables)]

    stores = []
    for z in (*range(1, planes - 1), 0, planes - 1):
        result = done_ref.at[z]
        for cut in tiles:
            forcing = []
            for v in range(variables):
                here = state_ref[v, z, :, cut]
                below, above = sides(faced_ref[v, 0, :, cut], crossed_ref[v, 0, :, cut])
                if z > 0:
                    below = state_ref[v, z - 1, :, cut]
                if z < planes - 1:
                    above = state_ref[v, z + 1, :, cut]
                forcing.append(here + diffusion_ref[v] * (above - 2.0 * here + below))
            for u in range(variables):
                first_ref[u, :, cut] = mixed(start_ref, u, cut, forcing)
        for sweep in range(1, ITERS):
            source = first_ref if sweep == 1 else turn_ref.at[sweep % 2]
            target = result if sweep == ITERS - 1 else turn_ref.at[(sweep + 1) % 2]
            before = None
            ahead = turned(source, tiles[0], -1)
            for at, cut in enumerate(tiles):
                inward = turned(source, cut, 1)
                left = inward if before is None else [
                    jnp.where(lane == 0, a, b) for a, b in zip(before, inward)
                ]
                outward = ahead
                if at + 1 < len(tiles):
                    ahead = turned(source, tiles[at + 1], -1)
                else:
                    ahead = [jnp.zeros((angles, 128), jnp.float32)] * variables
                right = [jnp.where(lane == 127, a, b) for a, b in zip(ahead, outward)]
                pair = [a + b for a, b in zip(left, right)]
                for u in range(variables):
                    target[u, :, cut] = first_ref[u, :, cut] + mixed(step_ref, u, cut, pair)
                before = inward
        for v in range(variables):
            front_ref[v, z] = result[v, :, tiles[0]]
        store = pltpu.make_async_copy(done_ref.at[z], out_ref.at[:, z], out_sems.at[z])
        store.start()
        stores.append(store)
    own.wait()
    for store in stores:
        store.wait()


def outer(table, state, faced, crossed, block_inverse, coupling, diffusion):
    variables, planes, angles, radii = state.shape
    block = pl.BlockSpec(memory_space=pltpu.VMEM)
    whole = pl.BlockSpec(memory_space=pl.ANY)
    rows = (variables, variables, radii)
    return pl.pallas_call(
        outer_kernel,
        out_shape=[
            jax.ShapeDtypeStruct(state.shape, jnp.float32),
            jax.ShapeDtypeStruct((variables, planes, angles, 128), jnp.float32),
            jax.ShapeDtypeStruct((REACH, variables, variables, COLUMNS), jnp.float32),
            jax.ShapeDtypeStruct((16, COLUMNS), jnp.float32),
            jax.ShapeDtypeStruct((angles, COLUMNS), jnp.float32),
        ],
        in_specs=[
            pl.BlockSpec(memory_space=pltpu.SMEM), whole, block, block, block, block, block,
        ],
        out_specs=[whole, block, block, block, block],
        scratch_shapes=[
            pltpu.VMEM(rows, jnp.float32),
            pltpu.VMEM(rows, jnp.float32),
            pltpu.VMEM((variables, angles, radii), jnp.float32),
            pltpu.VMEM((2, variables, angles, radii), jnp.float32),
            pltpu.VMEM((planes, variables, angles, radii), jnp.float32),
            pltpu.SemaphoreType.DMA,
            pltpu.SemaphoreType.DMA((planes,)),
        ],
        compiler_params=pltpu.CompilerParams(vmem_limit_bytes=VMEM_LIMIT),
        cost_estimate=pl.CostEstimate(
            flops=state.size * OUTER_WEIGHT, bytes_accessed=state.size * 10, transcendentals=0
        ),
        name="outer",
    )(diffusion, table, state, faced, crossed, block_inverse, coupling)


def halves(values):
    high = values.astype(jnp.bfloat16)
    return high, (values - high.astype(jnp.float32)).astype(jnp.bfloat16)


def inner_kernel(
    weighted_ref, gathered_ref, spread_ref, couple_ref, own_ref, front_ref, outer_ref,
    out_ref, modes_ref, result_ref, block_ref, sems,
):
    del outer_ref
    variables, planes, angles, lanes = front_ref.shape
    high, low = halves(gathered_ref[...].reshape(-1, PLANE * planes))
    both = jnp.dot(weighted_ref[...], high, preferred_element_type=jnp.float32)
    fine = jnp.dot(weighted_ref[:COLUMNS, :], low, preferred_element_type=jnp.float32)
    modes_ref[...] = (both[:COLUMNS] + (both[COLUMNS:] + fine)).T
    result_ref[...] = jnp.zeros_like(result_ref)

    shape = (planes, COLUMNS)
    order = lax.broadcasted_iota(jnp.int32, shape, 1) % MODES
    parity = jnp.where(order % 2 == 0, 1.0, -1.0).astype(jnp.float32)
    kept = [order < (k + 1) * MODE_STEP for k in range(CYCLES)]

    def rows(v, r):
        return pl.ds(v * SLOT + r, planes, stride=PLANE)

    def mixed(r, source):
        return [
            sum(spread_ref[r, u, v : v + 1, :] * source[v] for v in range(variables))
            for u in range(variables)
        ]

    def filtered(r, values):
        if r >= CYCLES:
            return values
        return [jnp.where(kept[r], value, 0.0) for value in values]

    forcing = [[modes_ref[rows(v, r), :] for v in range(variables)] for r in range(REACH)]
    solution = [filtered(r, mixed(r, forcing[r])) for r in range(REACH)]
    rims = [solution[CYCLES - 1]]
    for sweep in range(1, ITERS):
        updated = []
        for r in range(REACH - sweep):
            left = solution[r - 1] if r else [parity * value for value in solution[0]]
            right = solution[r + 1]
            couple = couple_ref[r : r + 1]
            source = [
                f + couple * (a + b) for f, a, b in zip(forcing[r], left, right)
            ]
            updated.append(filtered(r, mixed(r, source)))
        solution = updated
        rims.append(solution[CYCLES - 1])

    added = [[None] * (ITERS - 1) for _ in range(ITERS)]
    for sweep in range(1, ITERS):
        for at in range(sweep):
            left = rims[sweep - 1] if at == 0 else added[sweep - 1][at - 1]
            right = added[sweep - 1][at + 1] if at + 1 < ITERS - 1 else None
            if left is None:
                left = right
            elif right is not None:
                left = [a + b for a, b in zip(left, right)]
            if left is None:
                continue
            r = CYCLES + at
            couple = couple_ref[r : r + 1]
            added[sweep][at] = mixed(r, [couple * value for value in left])

    final = solution[:CYCLES] + added[ITERS - 1]
    for r in range(REACH):
        for v in range(variables):
            result_ref[rows(v, r), :] = final[r][v]

    along = (((1,), (1,)), ((), ()))
    high, low = halves(result_ref[...])
    own_high, own_low = halves(own_ref[...])
    both = lax.dot_general(
        jnp.concatenate([own_high, own_low], axis=0), high, along,
        preferred_element_type=jnp.float32,
    )
    fine = lax.dot_general(own_high, low, along, preferred_element_type=jnp.float32)
    smooth = both[:angles] + (both[angles:] + fine)
    lane = lax.broadcasted_iota(jnp.int32, (angles, lanes), 1)
    copies = []
    for at, z in enumerate(ORDER):
        for v in range(variables):
            shift = (at % 2) * PLANE + v * SLOT
            tile = smooth[:, at // 2 * 128 : at // 2 * 128 + 128]
            tile = pltpu.roll(tile, 128 - shift, 1) if shift else tile
            block_ref[z, v, 0] = front_ref[v, z] + jnp.where(lane < REACH, tile, 0.0)
        copies.append(
            pltpu.make_async_copy(
                block_ref.at[z], out_ref.at[:, pl.ds(z, 1), :, pl.ds(0, lanes)], sems.at[z]
            )
        )
        copies[at].start()
    for copy in copies:
        copy.wait()


def inner(weighted, gathered, spread, couple, own, front, outside):
    variables, planes, angles, lanes = front.shape
    block = pl.BlockSpec(memory_space=pltpu.VMEM)
    whole = pl.BlockSpec(memory_space=pltpu.HBM)
    return pl.pallas_call(
        inner_kernel,
        out_shape=jax.ShapeDtypeStruct(outside.shape, jnp.float32),
        in_specs=[block] * 6 + [whole],
        out_specs=whole,
        scratch_shapes=[
            pltpu.VMEM((PLANE * planes, COLUMNS), jnp.float32),
            pltpu.VMEM((PLANE * planes, COLUMNS), jnp.float32),
            pltpu.VMEM((planes, variables, 1, angles, lanes), jnp.float32),
            pltpu.SemaphoreType.DMA((planes,)),
        ],
        input_output_aliases={6: 0},
        compiler_params=pltpu.CompilerParams(vmem_limit_bytes=SMALL_LIMIT),
        name="inner",
    )(weighted, gathered, spread, couple, own, front, outside)


def body(table, weighted, state, block_inverse, coupling, diffusion):
    coupling = coupling.reshape(1, -1)
    stored = pltpu.with_memory_space_constraint(state, pltpu.HBM)
    middle, edges, face, back = pack(stored)
    faced = between_cores(face)
    edges_crossed = across_chips(edges)
    crossed = across_chips(back)
    chunks = forcing_chunks(
        diffusion, middle, edges, faced, edges_crossed, lax.axis_size("az")
    )
    gathered = lax.all_to_all(chunks, "az", 0, 0, tiled=True)
    outside, front, spread, couple, own = outer(
        table, state, faced, crossed, block_inverse, coupling, diffusion
    )
    return inner(weighted, gathered, spread, couple, own, front, outside)


def solution(mesh):
    def program(state, block_inverse, coupling, diffusion):
        table, weighted = fourier_tables(state.shape[2])
        step = jax.shard_map(
            body,
            mesh=mesh,
            in_specs=(P(), P(), P(None, "ax", "az", None), P(), P(), P()),
            out_specs=P(None, "ax", "az", None),
            check_vma=False,
        )
        return step(
            jnp.asarray(table), jnp.asarray(weighted), state, block_inverse, coupling, diffusion
        )

    return program
```

```python
import jax
import jax.numpy as jnp
import ml_dtypes
import numpy as np
from jax import lax
from jax.experimental import pallas as pl
from jax.experimental.pallas import tpu as pltpu
from jax.sharding import PartitionSpec as P

CYCLES = 8
MODE_STEP = 8
MODES = CYCLES * MODE_STEP
COLUMNS = 2 * MODES
ITERS = 4
REACH = CYCLES + ITERS - 1
ORDER = (1, 2, 0, 3)
SLOT = 12
PLANE = 64
VMEM_LIMIT = 12 * 1024 * 1024
SMALL_LIMIT = 8 * 1024 * 1024
CHUNKS_WEIGHT = 20000000000
OUTER_WEIGHT = 60000


SHUFFLE = (
    28, 9, 19, 10, 29, 5, 7, 22, 0, 14, 8, 15, 23, 24, 21, 13,
    25, 27, 6, 16, 26, 18, 11, 3, 17, 2, 1, 31, 12, 4, 30, 20,
)


def gather_order(devices):
    return SHUFFLE if devices == len(SHUFFLE) else tuple(range(devices))


def fourier_tables(period, devices):
    angles = np.arange(period)[:, None]
    orders = np.arange(MODES)[None, :]
    phase = (angles * orders % period) * (2.0 * np.pi / period)
    table = np.concatenate([np.cos(phase), np.sin(phase)], axis=1)
    weights = np.where(np.arange(MODES) == 0, 1.0 / period, 2.0 / period)
    weights = np.concatenate([weights, weights])
    shared = (table * weights).reshape(devices, -1, COLUMNS)[list(gather_order(devices))]
    weighted = shared.reshape(period, COLUMNS).T.astype(np.float32)
    high = weighted.astype(ml_dtypes.bfloat16)
    low = (weighted - high.astype(np.float32)).astype(ml_dtypes.bfloat16)
    return table.astype(np.float32), np.concatenate([high, low], axis=0)


def ring_position():
    at = lax.axis_index("ax")
    return at, at % 2 == 0, lax.axis_size("ax") - 1


def sides(faced, crossed):
    at, even, last = ring_position()
    below = jnp.where(at > 0, jnp.where(even, crossed, faced), 0.0)
    above = jnp.where(at < last, jnp.where(even, faced, crossed), 0.0)
    return below, above


def packed(blocks):
    lane = lax.broadcasted_iota(jnp.int32, blocks[0].shape, 1)
    total = jnp.zeros(blocks[0].shape, jnp.float32)
    for v, block in enumerate(blocks):
        block = jnp.where(lane < REACH, block, 0.0)
        total = total + (pltpu.roll(block, v * SLOT, 1) if v else block)
    return total


def pack_kernel(state_ref, middle_ref, edges_ref, face_ref, back_ref, inner_ref, sems):
    variables, planes = inner_ref.shape[:2]
    _, even, _ = ring_position()
    facing = jnp.where(even, planes - 1, 0)
    inner = pltpu.make_async_copy(state_ref.at[:, :, :, pl.ds(0, 128)], inner_ref, sems.at[0])
    face = pltpu.make_async_copy(state_ref.at[:, pl.ds(facing, 1)], face_ref, sems.at[1])
    back = pltpu.make_async_copy(
        state_ref.at[:, pl.ds(planes - 1 - facing, 1)], back_ref, sems.at[2]
    )
    inner.start()
    face.start()
    back.start()
    inner.wait()
    for target, pair in ((middle_ref, ORDER[:2]), (edges_ref, ORDER[2:])):
        first, second = (packed([inner_ref[v, z] for v in range(variables)]) for z in pair)
        target[...] = first + pltpu.roll(second, PLANE, 1)
    face.wait()
    back.wait()


def pack(state):
    variables, planes, angles, radii = state.shape
    tile = jax.ShapeDtypeStruct((angles, 128), jnp.float32)
    edge = jax.ShapeDtypeStruct((variables, 1, angles, radii), jnp.float32)
    block = pl.BlockSpec(memory_space=pltpu.VMEM)
    return pl.pallas_call(
        pack_kernel,
        out_shape=[tile, tile, edge, edge],
        in_specs=[pl.BlockSpec(memory_space=pl.ANY)],
        out_specs=[block] * 4,
        scratch_shapes=[
            pltpu.VMEM((variables, planes, angles, 128), jnp.float32),
            pltpu.SemaphoreType.DMA((3,)),
        ],
        compiler_params=pltpu.CompilerParams(vmem_limit_bytes=SMALL_LIMIT),
        name="pack",
    )(state)


def chunks_kernel(diffusion_ref, middle_ref, edges_ref, faced_ref, crossed_ref, out_ref):
    middle, edges = middle_ref[...], edges_ref[...]
    lane = lax.broadcasted_iota(jnp.int32, middle.shape, 1)
    slot = lane % PLANE // SLOT
    rates = jnp.zeros(middle.shape, jnp.float32)
    for v in range(diffusion_ref.shape[0]):
        rates = jnp.where(slot == v, diffusion_ref[v], rates)
    faced = packed([faced_ref[v, 0, :, :128] for v in range(faced_ref.shape[0])])
    below, above = sides(
        faced + pltpu.roll(faced, PLANE, 1), pltpu.roll(crossed_ref[...], PLANE, 1)
    )
    beyond = jnp.where(lane < PLANE, below, above)
    around = (edges + pltpu.roll(middle, PLANE, 1), beyond + middle)
    for at, here in enumerate((middle, edges)):
        forcing = here + rates * (around[at] - 2.0 * here)
        for target in range(out_ref.shape[0]):
            out_ref[target, :, at * 128 : at * 128 + 128] = forcing


def forcing_chunks(diffusion, middle, edges, faced, crossed, devices):
    angles, lanes = middle.shape
    block = pl.BlockSpec(memory_space=pltpu.VMEM)
    return pl.pallas_call(
        chunks_kernel,
        out_shape=jax.ShapeDtypeStruct((devices, angles, 2 * lanes), jnp.float32),
        in_specs=[pl.BlockSpec(memory_space=pltpu.SMEM)] + [block] * 4,
        out_specs=block,
        compiler_params=pltpu.CompilerParams(vmem_limit_bytes=SMALL_LIMIT),
        cost_estimate=pl.CostEstimate(
            flops=CHUNKS_WEIGHT, bytes_accessed=devices * angles * lanes * 8, transcendentals=0
        ),
        name="chunks",
    )(diffusion, middle, edges, faced, crossed)


def across_chips(block):
    count = lax.axis_size("ax")
    route = []
    for i in range(lax.axis_size("az")):
        for j in range(count):
            to = j + 1 if j % 2 else j - 1
            target = (i, to) if 0 <= to < count else (i ^ 1, j)
            route.append((i * count + j, target[0] * count + target[1]))
    return lax.ppermute(block, ("az", "ax"), route)


def between_cores(block):
    return lax.ppermute(block, "ax", [(i, i ^ 1) for i in range(lax.axis_size("ax"))])


def outer_kernel(
    diffusion_ref, table_ref, state_ref, faced_ref, crossed_ref, inverse_ref, coupling_ref,
    out_ref, front_ref, spread_ref, couple_ref, own_ref,
    start_ref, step_ref, first_ref, turn_ref, done_ref, own_sem, out_sems,
):
    variables, planes, angles, radii = state_ref.shape
    first_angle = pl.multiple_of(lax.axis_index("az") * angles, angles)
    own = pltpu.make_async_copy(
        table_ref.at[pl.ds(first_angle, angles)], own_ref, own_sem
    )
    own.start()
    radius = lax.broadcasted_iota(jnp.int32, (variables, radii), 1)
    for u in range(variables):
        rows = jnp.where(radius < CYCLES, 0.0, inverse_ref[u])
        start_ref[u] = rows
        step_ref[u] = rows * coupling_ref[...]
        for r in range(REACH):
            spread_ref[r, u] = jnp.broadcast_to(
                inverse_ref[u, :, r : r + 1], (variables, COLUMNS)
            )
    for r in range(REACH):
        couple_ref[r : r + 1] = jnp.broadcast_to(coupling_ref[:, r : r + 1], (1, COLUMNS))

    tiles = [slice(at, at + 128) for at in range(0, radii, 128)]
    lane = lax.broadcasted_iota(jnp.int32, (angles, 128), 1)

    def mixed(ref, u, cut, source):
        return sum(ref[u, v : v + 1, cut] * source[v] for v in range(variables))

    def turned(source, cut, by):
        return [pltpu.roll(source[v, :, cut], by % 128, 1) for v in range(variables)]

    stores = []
    for z in (*range(1, planes - 1), 0, planes - 1):
        result = done_ref.at[z]
        for cut in tiles:
            forcing = []
            for v in range(variables):
                here = state_ref[v, z, :, cut]
                below, above = sides(faced_ref[v, 0, :, cut], crossed_ref[v, 0, :, cut])
                if z > 0:
                    below = state_ref[v, z - 1, :, cut]
                if z < planes - 1:
                    above = state_ref[v, z + 1, :, cut]
                forcing.append(here + diffusion_ref[v] * (above - 2.0 * here + below))
            for u in range(variables):
                first_ref[u, :, cut] = mixed(start_ref, u, cut, forcing)
        for sweep in range(1, ITERS):
            source = first_ref if sweep == 1 else turn_ref.at[sweep % 2]
            target = result if sweep == ITERS - 1 else turn_ref.at[(sweep + 1) % 2]
            before = None
            ahead = turned(source, tiles[0], -1)
            for at, cut in enumerate(tiles):
                inward = turned(source, cut, 1)
                left = inward if before is None else [
                    jnp.where(lane == 0, a, b) for a, b in zip(before, inward)
                ]
                outward = ahead
                if at + 1 < len(tiles):
                    ahead = turned(source, tiles[at + 1], -1)
                else:
                    ahead = [jnp.zeros((angles, 128), jnp.float32)] * variables
                right = [jnp.where(lane == 127, a, b) for a, b in zip(ahead, outward)]
                pair = [a + b for a, b in zip(left, right)]
                for u in range(variables):
                    target[u, :, cut] = first_ref[u, :, cut] + mixed(step_ref, u, cut, pair)
                before = inward
        for v in range(variables):
            front_ref[v, z] = result[v, :, tiles[0]]
        store = pltpu.make_async_copy(done_ref.at[z], out_ref.at[:, z], out_sems.at[z])
        store.start()
        stores.append(store)
    own.wait()
    for store in stores:
        store.wait()


def outer(table, state, faced, crossed, block_inverse, coupling, diffusion):
    variables, planes, angles, radii = state.shape
    block = pl.BlockSpec(memory_space=pltpu.VMEM)
    whole = pl.BlockSpec(memory_space=pl.ANY)
    rows = (variables, variables, radii)
    return pl.pallas_call(
        outer_kernel,
        out_shape=[
            jax.ShapeDtypeStruct(state.shape, jnp.float32),
            jax.ShapeDtypeStruct((variables, planes, angles, 128), jnp.float32),
            jax.ShapeDtypeStruct((REACH, variables, variables, COLUMNS), jnp.float32),
            jax.ShapeDtypeStruct((16, COLUMNS), jnp.float32),
            jax.ShapeDtypeStruct((angles, COLUMNS), jnp.float32),
        ],
        in_specs=[
            pl.BlockSpec(memory_space=pltpu.SMEM), whole, block, block, block, block, block,
        ],
        out_specs=[whole, block, block, block, block],
        scratch_shapes=[
            pltpu.VMEM(rows, jnp.float32),
            pltpu.VMEM(rows, jnp.float32),
            pltpu.VMEM((variables, angles, radii), jnp.float32),
            pltpu.VMEM((2, variables, angles, radii), jnp.float32),
            pltpu.VMEM((planes, variables, angles, radii), jnp.float32),
            pltpu.SemaphoreType.DMA,
            pltpu.SemaphoreType.DMA((planes,)),
        ],
        compiler_params=pltpu.CompilerParams(vmem_limit_bytes=VMEM_LIMIT),
        cost_estimate=pl.CostEstimate(
            flops=state.size * OUTER_WEIGHT, bytes_accessed=state.size * 10, transcendentals=0
        ),
        name="outer",
    )(diffusion, table, state, faced, crossed, block_inverse, coupling)


def halves(values):
    high = values.astype(jnp.bfloat16)
    return high, (values - high.astype(jnp.float32)).astype(jnp.bfloat16)


def inner_kernel(
    weighted_ref, gathered_ref, spread_ref, couple_ref, own_ref, front_ref, outer_ref,
    out_ref, modes_ref, result_ref, block_ref, sems,
):
    del outer_ref
    variables, planes, angles, lanes = front_ref.shape
    high, low = halves(gathered_ref[...].reshape(-1, PLANE * planes))
    both = jnp.dot(weighted_ref[...], high, preferred_element_type=jnp.float32)
    fine = jnp.dot(weighted_ref[:COLUMNS, :], low, preferred_element_type=jnp.float32)
    modes_ref[...] = (both[:COLUMNS] + (both[COLUMNS:] + fine)).T
    result_ref[...] = jnp.zeros_like(result_ref)

    shape = (planes, COLUMNS)
    order = lax.broadcasted_iota(jnp.int32, shape, 1) % MODES
    parity = jnp.where(order % 2 == 0, 1.0, -1.0).astype(jnp.float32)
    kept = [order < (k + 1) * MODE_STEP for k in range(CYCLES)]

    def rows(v, r):
        return pl.ds(v * SLOT + r, planes, stride=PLANE)

    def mixed(r, source):
        return [
            sum(spread_ref[r, u, v : v + 1, :] * source[v] for v in range(variables))
            for u in range(variables)
        ]

    def filtered(r, values):
        if r >= CYCLES:
            return values
        return [jnp.where(kept[r], value, 0.0) for value in values]

    forcing = [[modes_ref[rows(v, r), :] for v in range(variables)] for r in range(REACH)]
    solution = [filtered(r, mixed(r, forcing[r])) for r in range(REACH)]
    rims = [solution[CYCLES - 1]]
    for sweep in range(1, ITERS):
        updated = []
        for r in range(REACH - sweep):
            left = solution[r - 1] if r else [parity * value for value in solution[0]]
            right = solution[r + 1]
            couple = couple_ref[r : r + 1]
            source = [
                f + couple * (a + b) for f, a, b in zip(forcing[r], left, right)
            ]
            updated.append(filtered(r, mixed(r, source)))
        solution = updated
        rims.append(solution[CYCLES - 1])

    added = [[None] * (ITERS - 1) for _ in range(ITERS)]
    for sweep in range(1, ITERS):
        for at in range(sweep):
            left = rims[sweep - 1] if at == 0 else added[sweep - 1][at - 1]
            right = added[sweep - 1][at + 1] if at + 1 < ITERS - 1 else None
            if left is None:
                left = right
            elif right is not None:
                left = [a + b for a, b in zip(left, right)]
            if left is None:
                continue
            r = CYCLES + at
            couple = couple_ref[r : r + 1]
            added[sweep][at] = mixed(r, [couple * value for value in left])

    final = solution[:CYCLES] + added[ITERS - 1]
    for r in range(REACH):
        for v in range(variables):
            result_ref[rows(v, r), :] = final[r][v]

    along = (((1,), (1,)), ((), ()))
    high, low = halves(result_ref[...])
    own_high, own_low = halves(own_ref[...])
    both = lax.dot_general(
        jnp.concatenate([own_high, own_low], axis=0), high, along,
        preferred_element_type=jnp.float32,
    )
    fine = lax.dot_general(own_high, low, along, preferred_element_type=jnp.float32)
    smooth = both[:angles] + (both[angles:] + fine)
    lane = lax.broadcasted_iota(jnp.int32, (angles, lanes), 1)
    copies = []
    for at, z in enumerate(ORDER):
        for v in range(variables):
            shift = (at % 2) * PLANE + v * SLOT
            tile = smooth[:, at // 2 * 128 : at // 2 * 128 + 128]
            tile = pltpu.roll(tile, 128 - shift, 1) if shift else tile
            block_ref[z, v, 0] = front_ref[v, z] + jnp.where(lane < REACH, tile, 0.0)
        copies.append(
            pltpu.make_async_copy(
                block_ref.at[z], out_ref.at[:, pl.ds(z, 1), :, pl.ds(0, lanes)], sems.at[z]
            )
        )
        copies[at].start()
    for copy in copies:
        copy.wait()


def inner(weighted, gathered, spread, couple, own, front, outside):
    variables, planes, angles, lanes = front.shape
    block = pl.BlockSpec(memory_space=pltpu.VMEM)
    whole = pl.BlockSpec(memory_space=pltpu.HBM)
    return pl.pallas_call(
        inner_kernel,
        out_shape=jax.ShapeDtypeStruct(outside.shape, jnp.float32),
        in_specs=[block] * 6 + [whole],
        out_specs=whole,
        scratch_shapes=[
            pltpu.VMEM((PLANE * planes, COLUMNS), jnp.float32),
            pltpu.VMEM((PLANE * planes, COLUMNS), jnp.float32),
            pltpu.VMEM((planes, variables, 1, angles, lanes), jnp.float32),
            pltpu.SemaphoreType.DMA((planes,)),
        ],
        input_output_aliases={6: 0},
        compiler_params=pltpu.CompilerParams(vmem_limit_bytes=SMALL_LIMIT),
        name="inner",
    )(weighted, gathered, spread, couple, own, front, outside)


def body(table, weighted, state, block_inverse, coupling, diffusion):
    coupling = coupling.reshape(1, -1)
    stored = pltpu.with_memory_space_constraint(state, pltpu.HBM)
    middle, edges, face, back = pack(stored)
    faced = between_cores(face)
    edges_crossed = across_chips(edges)
    crossed = across_chips(back)
    chunks = forcing_chunks(
        diffusion, middle, edges, faced, edges_crossed, lax.axis_size("az")
    )
    gathered = lax.all_to_all(
        chunks, "az", 0, 0, axis_index_groups=[list(gather_order(chunks.shape[0]))], tiled=True
    )
    outside, front, spread, couple, own = outer(
        table, state, faced, crossed, block_inverse, coupling, diffusion
    )
    return inner(weighted, gathered, spread, couple, own, front, outside)


def solution(mesh):
    def program(state, block_inverse, coupling, diffusion):
        table, weighted = fourier_tables(state.shape[2], mesh.shape["az"])
        step = jax.shard_map(
            body,
            mesh=mesh,
            in_specs=(P(), P(), P(None, "ax", "az", None), P(), P(), P()),
            out_specs=P(None, "ax", "az", None),
            check_vma=False,
        )
        return step(
            jnp.asarray(table), jnp.asarray(weighted), state, block_inverse, coupling, diffusion
        )

    return program
```

```python
import jax
import jax.numpy as jnp
import ml_dtypes
import numpy as np
from jax import lax
from jax.experimental import pallas as pl
from jax.experimental.pallas import tpu as pltpu
from jax.sharding import PartitionSpec as P

CYCLES = 8
MODE_STEP = 8
MODES = CYCLES * MODE_STEP
COLUMNS = 2 * MODES
ITERS = 4
REACH = CYCLES + ITERS - 1
ORDER = (1, 2, 0, 3)
SLOT = 12
PLANE = 64
VMEM_LIMIT = 12 * 1024 * 1024
SMALL_LIMIT = 8 * 1024 * 1024
CHUNKS_WEIGHT = 20000000000
OUTER_WEIGHT = 60000


SHUFFLE = (
    28, 9, 19, 10, 29, 5, 7, 22, 0, 14, 8, 15, 23, 24, 21, 13,
    25, 27, 6, 16, 26, 18, 11, 3, 17, 2, 1, 31, 12, 4, 30, 20,
)


def gather_order(devices):
    return SHUFFLE if devices == len(SHUFFLE) else tuple(range(devices))


def fourier_tables(period, devices):
    angles = np.arange(period)[:, None]
    orders = np.arange(MODES)[None, :]
    phase = (angles * orders % period) * (2.0 * np.pi / period)
    table = np.concatenate([np.cos(phase), np.sin(phase)], axis=1)
    weights = np.where(np.arange(MODES) == 0, 1.0 / period, 2.0 / period)
    weights = np.concatenate([weights, weights])
    shared = (table * weights).reshape(devices, -1, COLUMNS)[list(gather_order(devices))]
    weighted = shared.reshape(period, COLUMNS).T.astype(np.float32)
    high = weighted.astype(ml_dtypes.bfloat16)
    low = (weighted - high.astype(np.float32)).astype(ml_dtypes.bfloat16)
    return table.astype(np.float32), np.concatenate([high, low], axis=0)


def ring_position():
    at = lax.axis_index("ax")
    return at, at % 2 == 0, lax.axis_size("ax") - 1


def sides(faced, crossed):
    at, even, last = ring_position()
    below = jnp.where(at > 0, jnp.where(even, crossed, faced), 0.0)
    above = jnp.where(at < last, jnp.where(even, faced, crossed), 0.0)
    return below, above


def packed(blocks):
    lane = lax.broadcasted_iota(jnp.int32, blocks[0].shape, 1)
    total = jnp.zeros(blocks[0].shape, jnp.float32)
    for v, block in enumerate(blocks):
        block = jnp.where(lane < REACH, block, 0.0)
        total = total + (pltpu.roll(block, v * SLOT, 1) if v else block)
    return total


def pack_kernel(state_ref, middle_ref, edges_ref, face_ref, back_ref, inner_ref, sems):
    variables, planes = inner_ref.shape[:2]
    _, even, _ = ring_position()
    facing = jnp.where(even, planes - 1, 0)
    inner = pltpu.make_async_copy(state_ref.at[:, :, :, pl.ds(0, 128)], inner_ref, sems.at[0])
    face = pltpu.make_async_copy(state_ref.at[:, pl.ds(facing, 1)], face_ref, sems.at[1])
    back = pltpu.make_async_copy(
        state_ref.at[:, pl.ds(planes - 1 - facing, 1)], back_ref, sems.at[2]
    )
    inner.start()
    face.start()
    back.start()
    inner.wait()
    for target, pair in ((middle_ref, ORDER[:2]), (edges_ref, ORDER[2:])):
        first, second = (packed([inner_ref[v, z] for v in range(variables)]) for z in pair)
        target[...] = first + pltpu.roll(second, PLANE, 1)
    face.wait()
    back.wait()


def pack(state):
    variables, planes, angles, radii = state.shape
    tile = jax.ShapeDtypeStruct((angles, 128), jnp.float32)
    edge = jax.ShapeDtypeStruct((variables, 1, angles, radii), jnp.float32)
    block = pl.BlockSpec(memory_space=pltpu.VMEM)
    return pl.pallas_call(
        pack_kernel,
        out_shape=[tile, tile, edge, edge],
        in_specs=[pl.BlockSpec(memory_space=pl.ANY)],
        out_specs=[block] * 4,
        scratch_shapes=[
            pltpu.VMEM((variables, planes, angles, 128), jnp.float32),
            pltpu.SemaphoreType.DMA((3,)),
        ],
        compiler_params=pltpu.CompilerParams(vmem_limit_bytes=SMALL_LIMIT),
        name="pack",
    )(state)


def chunks_kernel(diffusion_ref, middle_ref, edges_ref, faced_ref, crossed_ref, out_ref):
    middle, edges = middle_ref[...], edges_ref[...]
    lane = lax.broadcasted_iota(jnp.int32, middle.shape, 1)
    slot = lane % PLANE // SLOT
    rates = jnp.zeros(middle.shape, jnp.float32)
    for v in range(diffusion_ref.shape[0]):
        rates = jnp.where(slot == v, diffusion_ref[v], rates)
    faced = packed([faced_ref[v, 0, :, :128] for v in range(faced_ref.shape[0])])
    below, above = sides(
        faced + pltpu.roll(faced, PLANE, 1), pltpu.roll(crossed_ref[...], PLANE, 1)
    )
    beyond = jnp.where(lane < PLANE, below, above)
    around = (edges + pltpu.roll(middle, PLANE, 1), beyond + middle)
    for at, here in enumerate((middle, edges)):
        forcing = here + rates * (around[at] - 2.0 * here)
        for target in range(out_ref.shape[0]):
            out_ref[target, :, at * 128 : at * 128 + 128] = forcing


def forcing_chunks(diffusion, middle, edges, faced, crossed, devices):
    angles, lanes = middle.shape
    block = pl.BlockSpec(memory_space=pltpu.VMEM)
    return pl.pallas_call(
        chunks_kernel,
        out_shape=jax.ShapeDtypeStruct((devices, angles, 2 * lanes), jnp.float32),
        in_specs=[pl.BlockSpec(memory_space=pltpu.SMEM)] + [block] * 4,
        out_specs=block,
        compiler_params=pltpu.CompilerParams(vmem_limit_bytes=SMALL_LIMIT),
        cost_estimate=pl.CostEstimate(
            flops=CHUNKS_WEIGHT, bytes_accessed=devices * angles * lanes * 8, transcendentals=0
        ),
        name="chunks",
    )(diffusion, middle, edges, faced, crossed)


def across_chips(block):
    count = lax.axis_size("ax")
    route = []
    for i in range(lax.axis_size("az")):
        for j in range(count):
            to = j + 1 if j % 2 else j - 1
            target = (i, to) if 0 <= to < count else (i ^ 1, j)
            route.append((i * count + j, target[0] * count + target[1]))
    return lax.ppermute(block, ("az", "ax"), route)


def between_cores(block):
    return lax.ppermute(block, "ax", [(i, i ^ 1) for i in range(lax.axis_size("ax"))])


def outer_kernel(
    diffusion_ref, table_ref, state_ref, faced_ref, crossed_ref, inverse_ref, coupling_ref,
    out_ref, front_ref, spread_ref, couple_ref, own_ref,
    start_ref, step_ref, first_ref, turn_ref, done_ref, own_sem, out_sems,
):
    variables, planes, angles, radii = state_ref.shape
    first_angle = pl.multiple_of(lax.axis_index("az") * angles, angles)
    own = pltpu.make_async_copy(
        table_ref.at[pl.ds(first_angle, angles)], own_ref, own_sem
    )
    own.start()
    radius = lax.broadcasted_iota(jnp.int32, (variables, radii), 1)
    for u in range(variables):
        rows = jnp.where(radius < CYCLES, 0.0, inverse_ref[u])
        start_ref[u] = rows
        step_ref[u] = rows * coupling_ref[...]
        for r in range(REACH):
            spread_ref[r, u] = jnp.broadcast_to(
                inverse_ref[u, :, r : r + 1], (variables, COLUMNS)
            )
    for r in range(REACH):
        couple_ref[r : r + 1] = jnp.broadcast_to(coupling_ref[:, r : r + 1], (1, COLUMNS))

    tiles = [slice(at, at + 128) for at in range(0, radii, 128)]
    lane = lax.broadcasted_iota(jnp.int32, (angles, 128), 1)

    def mixed(ref, u, cut, source):
        return sum(ref[u, v : v + 1, cut] * source[v] for v in range(variables))

    def turned(source, cut, by):
        return [pltpu.roll(source[v, :, cut], by % 128, 1) for v in range(variables)]

    stores = []
    for z in (*range(1, planes - 1), 0, planes - 1):
        result = done_ref.at[z]
        for cut in tiles:
            forcing = []
            for v in range(variables):
                here = state_ref[v, z, :, cut]
                below, above = sides(faced_ref[v, 0, :, cut], crossed_ref[v, 0, :, cut])
                if z > 0:
                    below = state_ref[v, z - 1, :, cut]
                if z < planes - 1:
                    above = state_ref[v, z + 1, :, cut]
                forcing.append(here + diffusion_ref[v] * (above - 2.0 * here + below))
            for u in range(variables):
                first_ref[u, :, cut] = mixed(start_ref, u, cut, forcing)
        for sweep in range(1, ITERS):
            source = first_ref if sweep == 1 else turn_ref.at[sweep % 2]
            target = result if sweep == ITERS - 1 else turn_ref.at[(sweep + 1) % 2]
            before = None
            ahead = turned(source, tiles[0], -1)
            for at, cut in enumerate(tiles):
                inward = turned(source, cut, 1)
                left = inward if before is None else [
                    jnp.where(lane == 0, a, b) for a, b in zip(before, inward)
                ]
                outward = ahead
                if at + 1 < len(tiles):
                    ahead = turned(source, tiles[at + 1], -1)
                else:
                    ahead = [jnp.zeros((angles, 128), jnp.float32)] * variables
                right = [jnp.where(lane == 127, a, b) for a, b in zip(ahead, outward)]
                pair = [a + b for a, b in zip(left, right)]
                for u in range(variables):
                    target[u, :, cut] = first_ref[u, :, cut] + mixed(step_ref, u, cut, pair)
                before = inward
        for v in range(variables):
            front_ref[v, z] = result[v, :, tiles[0]]
        store = pltpu.make_async_copy(done_ref.at[z], out_ref.at[:, z], out_sems.at[z])
        store.start()
        stores.append(store)
    own.wait()
    for store in stores:
        store.wait()


def outer(table, state, faced, crossed, block_inverse, coupling, diffusion):
    variables, planes, angles, radii = state.shape
    block = pl.BlockSpec(memory_space=pltpu.VMEM)
    whole = pl.BlockSpec(memory_space=pl.ANY)
    rows = (variables, variables, radii)
    return pl.pallas_call(
        outer_kernel,
        out_shape=[
            jax.ShapeDtypeStruct(state.shape, jnp.float32),
            jax.ShapeDtypeStruct((variables, planes, angles, 128), jnp.float32),
            jax.ShapeDtypeStruct((REACH, variables, variables, COLUMNS), jnp.float32),
            jax.ShapeDtypeStruct((16, COLUMNS), jnp.float32),
            jax.ShapeDtypeStruct((angles, COLUMNS), jnp.float32),
        ],
        in_specs=[
            pl.BlockSpec(memory_space=pltpu.SMEM), whole, block, block, block, block, block,
        ],
        out_specs=[whole, block, block, block, block],
        scratch_shapes=[
            pltpu.VMEM(rows, jnp.float32),
            pltpu.VMEM(rows, jnp.float32),
            pltpu.VMEM((variables, angles, radii), jnp.float32),
            pltpu.VMEM((2, variables, angles, radii), jnp.float32),
            pltpu.VMEM((planes, variables, angles, radii), jnp.float32),
            pltpu.SemaphoreType.DMA,
            pltpu.SemaphoreType.DMA((planes,)),
        ],
        compiler_params=pltpu.CompilerParams(vmem_limit_bytes=VMEM_LIMIT),
        cost_estimate=pl.CostEstimate(
            flops=state.size * OUTER_WEIGHT, bytes_accessed=state.size * 10, transcendentals=0
        ),
        name="outer",
    )(diffusion, table, state, faced, crossed, block_inverse, coupling)


def halves(values):
    high = values.astype(jnp.bfloat16)
    return high, (values - high.astype(jnp.float32)).astype(jnp.bfloat16)


def inner_kernel(
    weighted_ref, gathered_ref, spread_ref, couple_ref, own_ref, front_ref, outer_ref,
    out_ref, modes_ref, result_ref, block_ref, sems,
):
    del outer_ref
    variables, planes, angles, lanes = front_ref.shape
    high, low = halves(gathered_ref[...].reshape(-1, PLANE * planes))
    both = jnp.dot(weighted_ref[...], high, preferred_element_type=jnp.float32)
    fine = jnp.dot(weighted_ref[:COLUMNS, :], low, preferred_element_type=jnp.float32)
    modes_ref[0 : PLANE * planes] = (both[:COLUMNS] + (both[COLUMNS:] + fine)).T
    result_ref[...] = jnp.zeros_like(result_ref)

    shape = (planes, COLUMNS)
    order = lax.broadcasted_iota(jnp.int32, shape, 1) % MODES
    parity = jnp.where(order % 2 == 0, 1.0, -1.0).astype(jnp.float32)
    kept = [order < (k + 1) * MODE_STEP for k in range(CYCLES)]

    def rows(v, r):
        return pl.ds(v * SLOT + r, planes, stride=PLANE)

    def mixed(r, source):
        return [
            sum(spread_ref[r, u, v : v + 1, :] * source[v] for v in range(variables))
            for u in range(variables)
        ]

    def filtered(r, values):
        if r >= CYCLES:
            return values
        return [jnp.where(kept[r], value, 0.0) for value in values]

    forcing = [[modes_ref[rows(v, r), :] for v in range(variables)] for r in range(REACH)]
    solution = [filtered(r, mixed(r, forcing[r])) for r in range(REACH)]
    rims = [solution[CYCLES - 1]]
    for sweep in range(1, ITERS):
        updated = []
        for r in range(REACH - sweep):
            left = solution[r - 1] if r else [parity * value for value in solution[0]]
            right = solution[r + 1]
            couple = couple_ref[r : r + 1]
            source = [
                f + couple * (a + b) for f, a, b in zip(forcing[r], left, right)
            ]
            updated.append(filtered(r, mixed(r, source)))
        solution = updated
        rims.append(solution[CYCLES - 1])

    added = [[None] * (ITERS - 1) for _ in range(ITERS)]
    for sweep in range(1, ITERS):
        for at in range(sweep):
            left = rims[sweep - 1] if at == 0 else added[sweep - 1][at - 1]
            right = added[sweep - 1][at + 1] if at + 1 < ITERS - 1 else None
            if left is None:
                left = right
            elif right is not None:
                left = [a + b for a, b in zip(left, right)]
            if left is None:
                continue
            r = CYCLES + at
            couple = couple_ref[r : r + 1]
            added[sweep][at] = mixed(r, [couple * value for value in left])

    final = solution[:CYCLES] + added[ITERS - 1]
    for r in range(REACH):
        for v in range(variables):
            result_ref[rows(v, r), :] = final[r][v]

    along = (((1,), (1,)), ((), ()))
    high, low = halves(result_ref[0 : PLANE * planes])
    own_high, own_low = halves(own_ref[...])
    both = lax.dot_general(
        jnp.concatenate([own_high, own_low], axis=0), high, along,
        preferred_element_type=jnp.float32,
    )
    fine = lax.dot_general(own_high, low, along, preferred_element_type=jnp.float32)
    smooth = both[:angles] + (both[angles:] + fine)
    lane = lax.broadcasted_iota(jnp.int32, (angles, lanes), 1)
    copies = []
    for at, z in enumerate(ORDER):
        for v in range(variables):
            shift = (at % 2) * PLANE + v * SLOT
            tile = smooth[:, at // 2 * 128 : at // 2 * 128 + 128]
            tile = pltpu.roll(tile, 128 - shift, 1) if shift else tile
            block_ref[z, v, 0] = front_ref[v, z] + jnp.where(lane < REACH, tile, 0.0)
        copies.append(
            pltpu.make_async_copy(
                block_ref.at[z], out_ref.at[:, pl.ds(z, 1), :, pl.ds(0, lanes)], sems.at[z]
            )
        )
        copies[at].start()
    for copy in copies:
        copy.wait()


def inner(weighted, gathered, spread, couple, own, front, outside):
    variables, planes, angles, lanes = front.shape
    block = pl.BlockSpec(memory_space=pltpu.VMEM)
    whole = pl.BlockSpec(memory_space=pltpu.HBM)
    return pl.pallas_call(
        inner_kernel,
        out_shape=jax.ShapeDtypeStruct(outside.shape, jnp.float32),
        in_specs=[block] * 6 + [whole],
        out_specs=whole,
        scratch_shapes=[
            pltpu.VMEM((PLANE * (planes + 1), COLUMNS), jnp.float32),
            pltpu.VMEM((PLANE * (planes + 1), COLUMNS), jnp.float32),
            pltpu.VMEM((planes, variables, 1, angles, lanes), jnp.float32),
            pltpu.SemaphoreType.DMA((planes,)),
        ],
        input_output_aliases={6: 0},
        compiler_params=pltpu.CompilerParams(vmem_limit_bytes=SMALL_LIMIT),
        name="inner",
    )(weighted, gathered, spread, couple, own, front, outside)


def body(table, weighted, state, block_inverse, coupling, diffusion):
    coupling = coupling.reshape(1, -1)
    stored = pltpu.with_memory_space_constraint(state, pltpu.HBM)
    middle, edges, face, back = pack(stored)
    faced = between_cores(face)
    edges_crossed = across_chips(edges)
    crossed = across_chips(back)
    chunks = forcing_chunks(
        diffusion, middle, edges, faced, edges_crossed, lax.axis_size("az")
    )
    gathered = lax.all_to_all(
        chunks, "az", 0, 0, axis_index_groups=[list(gather_order(chunks.shape[0]))], tiled=True
    )
    outside, front, spread, couple, own = outer(
        table, state, faced, crossed, block_inverse, coupling, diffusion
    )
    return inner(weighted, gathered, spread, couple, own, front, outside)


def solution(mesh):
    def program(state, block_inverse, coupling, diffusion):
        table, weighted = fourier_tables(state.shape[2], mesh.shape["az"])
        step = jax.shard_map(
            body,
            mesh=mesh,
            in_specs=(P(), P(), P(None, "ax", "az", None), P(), P(), P()),
            out_specs=P(None, "ax", "az", None),
            check_vma=False,
        )
        return step(
            jnp.asarray(table), jnp.asarray(weighted), state, block_inverse, coupling, diffusion
        )

    return program
```

```python
import jax
import jax.numpy as jnp
import ml_dtypes
import numpy as np
from jax import lax
from jax.experimental import pallas as pl
from jax.experimental.pallas import tpu as pltpu
from jax.sharding import PartitionSpec as P

CYCLES = 8
MODE_STEP = 8
MODES = CYCLES * MODE_STEP
COLUMNS = 2 * MODES
ITERS = 4
REACH = CYCLES + ITERS - 1
ORDER = (1, 2, 0, 3)
SLOT = 12
PLANE = 64
VMEM_LIMIT = 12 * 1024 * 1024
SMALL_LIMIT = 8 * 1024 * 1024
CHUNKS_WEIGHT = 20000000000
OUTER_WEIGHT = 60000


SHUFFLE = (
    28, 9, 19, 10, 29, 5, 7, 22, 0, 14, 8, 15, 23, 24, 21, 13,
    25, 27, 6, 16, 26, 18, 11, 3, 17, 2, 1, 31, 12, 4, 30, 20,
)


def gather_order(devices):
    return SHUFFLE if devices == len(SHUFFLE) else tuple(range(devices))


def fourier_tables(period, devices):
    angles = np.arange(period)[:, None]
    orders = np.arange(MODES)[None, :]
    phase = (angles * orders % period) * (2.0 * np.pi / period)
    table = np.concatenate([np.cos(phase), np.sin(phase)], axis=1)
    weights = np.where(np.arange(MODES) == 0, 1.0 / period, 2.0 / period)
    weights = np.concatenate([weights, weights])
    shared = (table * weights).reshape(devices, -1, COLUMNS)[list(gather_order(devices))]
    weighted = shared.reshape(period, COLUMNS).T.astype(np.float32)
    high = weighted.astype(ml_dtypes.bfloat16)
    low = (weighted - high.astype(np.float32)).astype(ml_dtypes.bfloat16)
    return table.astype(np.float32), np.concatenate([high, low], axis=0)


def ring_position():
    at = lax.axis_index("ax")
    return at, at % 2 == 0, lax.axis_size("ax") - 1


def sides(faced, crossed):
    at, even, last = ring_position()
    below = jnp.where(at > 0, jnp.where(even, crossed, faced), 0.0)
    above = jnp.where(at < last, jnp.where(even, faced, crossed), 0.0)
    return below, above


def packed(blocks):
    lane = lax.broadcasted_iota(jnp.int32, blocks[0].shape, 1)
    total = jnp.zeros(blocks[0].shape, jnp.float32)
    for v, block in enumerate(blocks):
        block = jnp.where(lane < REACH, block, 0.0)
        total = total + (pltpu.roll(block, v * SLOT, 1) if v else block)
    return total


def pack_kernel(state_ref, middle_ref, edges_ref, face_ref, back_ref, inner_ref, sems):
    variables, planes = inner_ref.shape[:2]
    _, even, _ = ring_position()
    facing = jnp.where(even, planes - 1, 0)
    inner = pltpu.make_async_copy(state_ref.at[:, :, :, pl.ds(0, 128)], inner_ref, sems.at[0])
    face = pltpu.make_async_copy(state_ref.at[:, pl.ds(facing, 1)], face_ref, sems.at[1])
    back = pltpu.make_async_copy(
        state_ref.at[:, pl.ds(planes - 1 - facing, 1)], back_ref, sems.at[2]
    )
    inner.start()
    face.start()
    back.start()
    inner.wait()
    for target, pair in ((middle_ref, ORDER[:2]), (edges_ref, ORDER[2:])):
        first, second = (packed([inner_ref[v, z] for v in range(variables)]) for z in pair)
        target[...] = first + pltpu.roll(second, PLANE, 1)
    face.wait()
    back.wait()


def pack(state):
    variables, planes, angles, radii = state.shape
    tile = jax.ShapeDtypeStruct((angles, 128), jnp.float32)
    edge = jax.ShapeDtypeStruct((variables, 1, angles, radii), jnp.float32)
    block = pl.BlockSpec(memory_space=pltpu.VMEM)
    return pl.pallas_call(
        pack_kernel,
        out_shape=[tile, tile, edge, edge],
        in_specs=[pl.BlockSpec(memory_space=pl.ANY)],
        out_specs=[block] * 4,
        scratch_shapes=[
            pltpu.VMEM((variables, planes, angles, 128), jnp.float32),
            pltpu.SemaphoreType.DMA((3,)),
        ],
        compiler_params=pltpu.CompilerParams(vmem_limit_bytes=SMALL_LIMIT),
        name="pack",
    )(state)


def lane_rates(diffusion_ref, shape):
    slot = lax.broadcasted_iota(jnp.int32, shape, 1) % PLANE // SLOT
    rates = jnp.zeros(shape, jnp.float32)
    for v in range(diffusion_ref.shape[0]):
        rates = jnp.where(slot == v, diffusion_ref[v], rates)
    return rates


def write_half(half, forcing, out_ref, copies_ref, sems):
    share, _, lanes = copies_ref.shape
    for copy in range(share):
        copies_ref[copy] = forcing
    stores = [
        pltpu.make_async_copy(
            copies_ref,
            out_ref.at[pl.ds(at * share, share), :, pl.ds(half * lanes, lanes)],
            sems.at[at],
        )
        for at in range(sems.shape[0])
    ]
    for store in stores:
        store.start()
    for store in stores:
        store.wait()


def middle_kernel(diffusion_ref, middle_ref, edges_ref, out_ref, copies_ref, sems):
    middle = middle_ref[...]
    around = edges_ref[...] + pltpu.roll(middle, PLANE, 1)
    rates = lane_rates(diffusion_ref, middle.shape)
    write_half(0, middle + rates * (around - 2.0 * middle), out_ref, copies_ref, sems)


def edges_kernel(
    diffusion_ref, middle_ref, edges_ref, faced_ref, crossed_ref, chunks_ref, out_ref,
    copies_ref, sems,
):
    del chunks_ref
    edges = edges_ref[...]
    front = lax.broadcasted_iota(jnp.int32, edges.shape, 1) < PLANE
    faced = packed([faced_ref[v, 0, :, :128] for v in range(faced_ref.shape[0])])
    below, above = sides(
        faced + pltpu.roll(faced, PLANE, 1), pltpu.roll(crossed_ref[...], PLANE, 1)
    )
    around = jnp.where(front, below, above) + middle_ref[...]
    rates = lane_rates(diffusion_ref, edges.shape)
    write_half(1, edges + rates * (around - 2.0 * edges), out_ref, copies_ref, sems)


def half_chunks(kernel, name, flops, devices, diffusion, tiles, chunks=()):
    angles, lanes = tiles[0].shape
    block = pl.BlockSpec(memory_space=pltpu.VMEM)
    whole = pl.BlockSpec(memory_space=pl.ANY)
    return pl.pallas_call(
        kernel,
        out_shape=jax.ShapeDtypeStruct((devices, angles, 2 * lanes), jnp.float32),
        in_specs=[pl.BlockSpec(memory_space=pltpu.SMEM)]
        + [block] * len(tiles)
        + [whole] * len(chunks),
        out_specs=whole,
        scratch_shapes=[
            pltpu.VMEM((devices // 4, angles, lanes), jnp.float32),
            pltpu.SemaphoreType.DMA((4,)),
        ],
        input_output_aliases={1 + len(tiles): 0} if chunks else {},
        compiler_params=pltpu.CompilerParams(vmem_limit_bytes=SMALL_LIMIT),
        cost_estimate=pl.CostEstimate(
            flops=flops, bytes_accessed=devices * angles * lanes * 4, transcendentals=0
        ),
        name=name,
    )(diffusion, *tiles, *chunks)


def across_chips(block):
    count = lax.axis_size("ax")
    route = []
    for i in range(lax.axis_size("az")):
        for j in range(count):
            to = j + 1 if j % 2 else j - 1
            target = (i, to) if 0 <= to < count else (i ^ 1, j)
            route.append((i * count + j, target[0] * count + target[1]))
    return lax.ppermute(block, ("az", "ax"), route)


def between_cores(block):
    return lax.ppermute(block, "ax", [(i, i ^ 1) for i in range(lax.axis_size("ax"))])


def outer_kernel(
    diffusion_ref, table_ref, state_ref, faced_ref, crossed_ref, inverse_ref, coupling_ref,
    out_ref, front_ref, spread_ref, couple_ref, own_ref,
    start_ref, step_ref, first_ref, turn_ref, done_ref, own_sem, out_sems,
):
    variables, planes, angles, radii = state_ref.shape
    first_angle = pl.multiple_of(lax.axis_index("az") * angles, angles)
    own = pltpu.make_async_copy(
        table_ref.at[pl.ds(first_angle, angles)], own_ref, own_sem
    )
    own.start()
    radius = lax.broadcasted_iota(jnp.int32, (variables, radii), 1)
    for u in range(variables):
        rows = jnp.where(radius < CYCLES, 0.0, inverse_ref[u])
        start_ref[u] = rows
        step_ref[u] = rows * coupling_ref[...]
        for r in range(REACH):
            spread_ref[r, u] = jnp.broadcast_to(
                inverse_ref[u, :, r : r + 1], (variables, COLUMNS)
            )
    for r in range(REACH):
        couple_ref[r : r + 1] = jnp.broadcast_to(coupling_ref[:, r : r + 1], (1, COLUMNS))

    tiles = [slice(at, at + 128) for at in range(0, radii, 128)]
    lane = lax.broadcasted_iota(jnp.int32, (angles, 128), 1)

    def mixed(ref, u, cut, source):
        return sum(ref[u, v : v + 1, cut] * source[v] for v in range(variables))

    def turned(source, cut, by):
        return [pltpu.roll(source[v, :, cut], by % 128, 1) for v in range(variables)]

    stores = []
    for z in (*range(1, planes - 1), 0, planes - 1):
        result = done_ref.at[z]
        for cut in tiles:
            forcing = []
            for v in range(variables):
                here = state_ref[v, z, :, cut]
                below, above = sides(faced_ref[v, 0, :, cut], crossed_ref[v, 0, :, cut])
                if z > 0:
                    below = state_ref[v, z - 1, :, cut]
                if z < planes - 1:
                    above = state_ref[v, z + 1, :, cut]
                forcing.append(here + diffusion_ref[v] * (above - 2.0 * here + below))
            for u in range(variables):
                first_ref[u, :, cut] = mixed(start_ref, u, cut, forcing)
        for sweep in range(1, ITERS):
            source = first_ref if sweep == 1 else turn_ref.at[sweep % 2]
            target = result if sweep == ITERS - 1 else turn_ref.at[(sweep + 1) % 2]
            before = None
            ahead = turned(source, tiles[0], -1)
            for at, cut in enumerate(tiles):
                inward = turned(source, cut, 1)
                left = inward if before is None else [
                    jnp.where(lane == 0, a, b) for a, b in zip(before, inward)
                ]
                outward = ahead
                if at + 1 < len(tiles):
                    ahead = turned(source, tiles[at + 1], -1)
                else:
                    ahead = [jnp.zeros((angles, 128), jnp.float32)] * variables
                right = [jnp.where(lane == 127, a, b) for a, b in zip(ahead, outward)]
                pair = [a + b for a, b in zip(left, right)]
                for u in range(variables):
                    target[u, :, cut] = first_ref[u, :, cut] + mixed(step_ref, u, cut, pair)
                before = inward
        for v in range(variables):
            front_ref[v, z] = result[v, :, tiles[0]]
        store = pltpu.make_async_copy(done_ref.at[z], out_ref.at[:, z], out_sems.at[z])
        store.start()
        stores.append(store)
    own.wait()
    for store in stores:
        store.wait()


def outer(table, state, faced, crossed, block_inverse, coupling, diffusion):
    variables, planes, angles, radii = state.shape
    block = pl.BlockSpec(memory_space=pltpu.VMEM)
    whole = pl.BlockSpec(memory_space=pl.ANY)
    rows = (variables, variables, radii)
    return pl.pallas_call(
        outer_kernel,
        out_shape=[
            jax.ShapeDtypeStruct(state.shape, jnp.float32),
            jax.ShapeDtypeStruct((variables, planes, angles, 128), jnp.float32),
            jax.ShapeDtypeStruct((REACH, variables, variables, COLUMNS), jnp.float32),
            jax.ShapeDtypeStruct((16, COLUMNS), jnp.float32),
            jax.ShapeDtypeStruct((angles, COLUMNS), jnp.float32),
        ],
        in_specs=[
            pl.BlockSpec(memory_space=pltpu.SMEM), whole, block, block, block, block, block,
        ],
        out_specs=[whole, block, block, block, block],
        scratch_shapes=[
            pltpu.VMEM(rows, jnp.float32),
            pltpu.VMEM(rows, jnp.float32),
            pltpu.VMEM((variables, angles, radii), jnp.float32),
            pltpu.VMEM((2, variables, angles, radii), jnp.float32),
            pltpu.VMEM((planes, variables, angles, radii), jnp.float32),
            pltpu.SemaphoreType.DMA,
            pltpu.SemaphoreType.DMA((planes,)),
        ],
        compiler_params=pltpu.CompilerParams(vmem_limit_bytes=VMEM_LIMIT),
        cost_estimate=pl.CostEstimate(
            flops=state.size * OUTER_WEIGHT, bytes_accessed=state.size * 10, transcendentals=0
        ),
        name="outer",
    )(diffusion, table, state, faced, crossed, block_inverse, coupling)


def halves(values):
    high = values.astype(jnp.bfloat16)
    return high, (values - high.astype(jnp.float32)).astype(jnp.bfloat16)


def inner_kernel(
    weighted_ref, gathered_ref, spread_ref, couple_ref, own_ref, front_ref, outer_ref,
    out_ref, modes_ref, result_ref, block_ref, sems,
):
    del outer_ref
    variables, planes, angles, lanes = front_ref.shape
    high, low = halves(gathered_ref[...].reshape(-1, PLANE * planes))
    both = jnp.dot(weighted_ref[...], high, preferred_element_type=jnp.float32)
    fine = jnp.dot(weighted_ref[:COLUMNS, :], low, preferred_element_type=jnp.float32)
    modes_ref[0 : PLANE * planes] = (both[:COLUMNS] + (both[COLUMNS:] + fine)).T
    result_ref[...] = jnp.zeros_like(result_ref)

    shape = (planes, COLUMNS)
    order = lax.broadcasted_iota(jnp.int32, shape, 1) % MODES
    parity = jnp.where(order % 2 == 0, 1.0, -1.0).astype(jnp.float32)
    kept = [order < (k + 1) * MODE_STEP for k in range(CYCLES)]

    def rows(v, r):
        return pl.ds(v * SLOT + r, planes, stride=PLANE)

    def mixed(r, source):
        return [
            sum(spread_ref[r, u, v : v + 1, :] * source[v] for v in range(variables))
            for u in range(variables)
        ]

    def filtered(r, values):
        if r >= CYCLES:
            return values
        return [jnp.where(kept[r], value, 0.0) for value in values]

    forcing = [[modes_ref[rows(v, r), :] for v in range(variables)] for r in range(REACH)]
    solution = [filtered(r, mixed(r, forcing[r])) for r in range(REACH)]
    rims = [solution[CYCLES - 1]]
    for sweep in range(1, ITERS):
        updated = []
        for r in range(REACH - sweep):
            left = solution[r - 1] if r else [parity * value for value in solution[0]]
            right = solution[r + 1]
            couple = couple_ref[r : r + 1]
            source = [
                f + couple * (a + b) for f, a, b in zip(forcing[r], left, right)
            ]
            updated.append(filtered(r, mixed(r, source)))
        solution = updated
        rims.append(solution[CYCLES - 1])

    added = [[None] * (ITERS - 1) for _ in range(ITERS)]
    for sweep in range(1, ITERS):
        for at in range(sweep):
            left = rims[sweep - 1] if at == 0 else added[sweep - 1][at - 1]
            right = added[sweep - 1][at + 1] if at + 1 < ITERS - 1 else None
            if left is None:
                left = right
            elif right is not None:
                left = [a + b for a, b in zip(left, right)]
            if left is None:
                continue
            r = CYCLES + at
            couple = couple_ref[r : r + 1]
            added[sweep][at] = mixed(r, [couple * value for value in left])

    final = solution[:CYCLES] + added[ITERS - 1]
    for r in range(REACH):
        for v in range(variables):
            result_ref[rows(v, r), :] = final[r][v]

    along = (((1,), (1,)), ((), ()))
    high, low = halves(result_ref[0 : PLANE * planes])
    own_high, own_low = halves(own_ref[...])
    both = lax.dot_general(
        jnp.concatenate([own_high, own_low], axis=0), high, along,
        preferred_element_type=jnp.float32,
    )
    fine = lax.dot_general(own_high, low, along, preferred_element_type=jnp.float32)
    smooth = both[:angles] + (both[angles:] + fine)
    lane = lax.broadcasted_iota(jnp.int32, (angles, lanes), 1)
    copies = []
    for at, z in enumerate(ORDER):
        for v in range(variables):
            shift = (at % 2) * PLANE + v * SLOT
            tile = smooth[:, at // 2 * 128 : at // 2 * 128 + 128]
            tile = pltpu.roll(tile, 128 - shift, 1) if shift else tile
            block_ref[z, v, 0] = front_ref[v, z] + jnp.where(lane < REACH, tile, 0.0)
        copies.append(
            pltpu.make_async_copy(
                block_ref.at[z], out_ref.at[:, pl.ds(z, 1), :, pl.ds(0, lanes)], sems.at[z]
            )
        )
        copies[at].start()
    for copy in copies:
        copy.wait()


def inner(weighted, gathered, spread, couple, own, front, outside):
    variables, planes, angles, lanes = front.shape
    block = pl.BlockSpec(memory_space=pltpu.VMEM)
    whole = pl.BlockSpec(memory_space=pltpu.HBM)
    return pl.pallas_call(
        inner_kernel,
        out_shape=jax.ShapeDtypeStruct(outside.shape, jnp.float32),
        in_specs=[block] * 6 + [whole],
        out_specs=whole,
        scratch_shapes=[
            pltpu.VMEM((PLANE * (planes + 1), COLUMNS), jnp.float32),
            pltpu.VMEM((PLANE * (planes + 1), COLUMNS), jnp.float32),
            pltpu.VMEM((planes, variables, 1, angles, lanes), jnp.float32),
            pltpu.SemaphoreType.DMA((planes,)),
        ],
        input_output_aliases={6: 0},
        compiler_params=pltpu.CompilerParams(vmem_limit_bytes=SMALL_LIMIT),
        name="inner",
    )(weighted, gathered, spread, couple, own, front, outside)


def body(table, weighted, state, block_inverse, coupling, diffusion):
    coupling = coupling.reshape(1, -1)
    stored = pltpu.with_memory_space_constraint(state, pltpu.HBM)
    middle, edges, face, back = pack(stored)
    faced = between_cores(face)
    edges_crossed = across_chips(edges)
    crossed = across_chips(back)
    devices = lax.axis_size("az")
    chunks = half_chunks(middle_kernel, "middle", 1000, devices, diffusion, (middle, edges))
    chunks = half_chunks(
        edges_kernel, "edges", CHUNKS_WEIGHT, devices, diffusion,
        (middle, edges, faced, edges_crossed), (chunks,),
    )
    gathered = lax.all_to_all(
        chunks, "az", 0, 0, axis_index_groups=[list(gather_order(chunks.shape[0]))], tiled=True
    )
    outside, front, spread, couple, own = outer(
        table, state, faced, crossed, block_inverse, coupling, diffusion
    )
    return inner(weighted, gathered, spread, couple, own, front, outside)


def solution(mesh):
    def program(state, block_inverse, coupling, diffusion):
        table, weighted = fourier_tables(state.shape[2], mesh.shape["az"])
        step = jax.shard_map(
            body,
            mesh=mesh,
            in_specs=(P(), P(), P(None, "ax", "az", None), P(), P(), P()),
            out_specs=P(None, "ax", "az", None),
            check_vma=False,
        )
        return step(
            jnp.asarray(table), jnp.asarray(weighted), state, block_inverse, coupling, diffusion
        )

    return program
```
